32 devices in a mesh: seq: 8 (over z, x), exp: 4 (over y, core).
Axes of the slice: x: 2, y: 2, z: 4, core: 2. Of those that a mesh axis runs over, the one named last changes fastest.
Arguments:
- queries: bfloat16 [2048, 2048], P('seq', 'exp'), may hold values from -112 to 112
- key_rows: bfloat16 [2048, 2048], P('seq', 'exp'), may hold values from -4 to 4
- value_rows: bfloat16 [2048, 2048], P('seq', 'exp'), may hold values from -6 to 6
- out_grad: bfloat16 [2048, 2048], P('seq', 'exp'), may hold values from -6 to 6
- expert_ids: int32 [2048, 2], P('seq'), may hold values from 0 to 7, all different within a row
- gate_values: float32 [2048, 2], P('seq'), may hold values from 0.1 to 1
- alibi_slope: float32 [16], P('exp'), may hold values from 0.00012207031 to 0.1
- expert_in: bfloat16 [8, 2048, 4096], P('seq', None, 'exp'), may hold values from -0.125 to 0.125
- expert_out: bfloat16 [8, 4096, 2048], P('seq', 'exp'), may hold values from -0.09375 to 0.09375
Outputs:
- query_grad: bfloat16 [2048, 2048], P('seq', 'exp')
- key_grad: bfloat16 [2048, 2048], P('seq', 'exp')
- value_grad: bfloat16 [2048, 2048], P('seq', 'exp')
- expert_in_grad: bfloat16 [8, 2048, 4096], P('seq', None, 'exp')
- expert_out_grad: bfloat16 [8, 4096, 2048], P('seq', 'exp')
The draws below stay inside these ranges and needn't reach their ends.
Inputs may be any that keep to these rules, and one draw needn't show every extreme that they name: `expert_ids`: each token names two different experts.
All inputs are finite; a program needn't handle non-finite values.
Results may differ from the reference program's by a relative error of at most 0.024.
Values may be sent and summed in bfloat16 or wider, within the bound.
No kernel may reach another device: no remote copies, remote signals or barrier semaphores. Data moves between devices by JAX's collectives and lax.ppermute only.
A program may use at most 128 MiB of HBM per device.

```python
import math
import jax
import jax.numpy as jnp
from jax import lax

D = 2048
H = 16
HD = 128
FF = 4096
BLOCK = 256
WCH = 16
EXPERTS = 8
CAP = 80
TOKENS = 2048
N_SEQ = 8
N_EXP = 4


def drawn_pair(key):
    base_keys = jnp.clip(jax.random.normal(jax.random.fold_in(key, 11), (TOKENS, D), jnp.float32), -4.0, 4.0)
    base_queries = jnp.clip(jax.random.normal(jax.random.fold_in(key, 12), (TOKENS, D), jnp.float32), -4.0, 4.0)
    return (base_queries, base_keys)


def draw_queries(key, part):
    return drawn_pair(key)[0].astype(jnp.bfloat16)


def draw_key_rows(key, part):
    return drawn_pair(key)[1].astype(jnp.bfloat16)


def steps_of(rng, dims, pieces, low, high):
    gain, own = 1.0, jax.random.fold_in(rng, 6)
    for axis_at, shards_of in pieces:
        draws = jnp.exp(jax.random.uniform(jax.random.fold_in(own, axis_at), (shards_of,), jnp.float32, low / len(pieces), high / len(pieces)))
        gain = gain * jnp.repeat(draws, dims[axis_at] // shards_of).reshape([-1 if axis == axis_at else 1 for axis in range(len(dims))])
    return gain


def picks_of(stream_key, rows, number_of, top, lift):
    order = jax.random.permutation(jax.random.fold_in(stream_key, 1), number_of)
    pull = order
    for power in range(3):
        pull = pull * pull // number_of
    pull = pull * lift // number_of
    chance = jax.random.randint(jax.random.fold_in(stream_key, 2), (rows, number_of), 0, 4096) + pull
    fixed_rows = jax.random.permutation(jax.random.fold_in(stream_key, 3), rows)[jnp.arange(number_of) % rows]
    chance = jnp.where(jnp.arange(rows)[:, None] == fixed_rows[None, :], 1 << 14, chance)
    priority = chance * number_of + jnp.arange(number_of)
    return lax.top_k(priority.astype(jnp.int32), top)[1].astype(jnp.int32)


def gaussian(stream_key, extent, deviation, limit, shards=(), held_as=jnp.bfloat16):
    array = deviation * jax.random.normal(stream_key, extent, jnp.float32)
    if shards:
        array = array * steps_of(stream_key, extent, shards, -0.22, 0.18)
    return jnp.clip(array, -limit, limit).astype(held_as)


def setup_inputs(seed: int = 0) -> dict:
    seeds = jax.random.split(jax.random.key(seed), 10)
    return {
        "queries": draw_queries(jax.random.fold_in(seeds[9], 71), 0),
        "key_rows": draw_key_rows(jax.random.fold_in(seeds[9], 71), 0),
        "value_rows": gaussian(seeds[2], (TOKENS, D), 1.0, 6.0, ((0, 8), (1, 4))),
        "out_grad": gaussian(seeds[3], (TOKENS, D), 1.0, 6.0, ((0, 8), (1, 4))),
        "expert_ids": picks_of(seeds[4], TOKENS, EXPERTS, 2, 4096),
        "gate_values": jnp.clip(0.1 + 0.9 * jax.random.uniform(seeds[5], (TOKENS, 2), jnp.float32) ** steps_of(seeds[5], (TOKENS, 2), ((0, 8),), -0.2, 0.2), 0.1, 1.0),
        "alibi_slope": jnp.clip(jnp.exp(math.log(0.1) - 6.7083283 * jax.random.uniform(seeds[6], (H,), jnp.float32) ** steps_of(seeds[6], (H,), ((0, 4),), -0.2, 0.2)), 0.00012207031, 0.1),
        "expert_in": gaussian(seeds[7], (EXPERTS, D, FF), D ** -0.5, 0.125, ((0, 8), (2, 4))),
        "expert_out": gaussian(seeds[8], (EXPERTS, FF, D), FF ** -0.5, 0.09375, ((0, 8), (1, 4))),
    }


def block_scores(query_heads, key_block, slopes, first_valid, window):
    raw_scores = jnp.einsum("ihd,jhd->hij", query_heads.astype(jnp.float32), key_block.astype(jnp.float32)) * (HD ** -0.5)
    row_pos = lax.broadcasted_iota(jnp.int32, (query_heads.shape[0], key_block.shape[0]), 0)
    col_pos = lax.broadcasted_iota(jnp.int32, (query_heads.shape[0], key_block.shape[0]), 1)
    distance = row_pos - col_pos + window
    in_window = (distance >= 0) & (distance < window) & (col_pos >= first_valid)
    biased = raw_scores - slopes[:, None, None] * distance.astype(jnp.float32)[None]
    return jnp.where(in_window[None], biased, -jnp.inf)


def slot_positions(flat_ids):
    expert_cols = lax.broadcasted_iota(jnp.int32, flat_ids.shape + (EXPERTS,), 2)
    one_hot = (flat_ids[..., None] == expert_cols).astype(jnp.int32)
    before = jnp.cumsum(one_hot, axis=1) - one_hot
    return jnp.sum(before * one_hot, axis=2).astype(jnp.int32)


def reference(queries, key_rows, value_rows, out_grad, expert_ids, gate_values, alibi_slope, expert_in, expert_out):
    score_scale = HD ** -0.5
    window = WCH * BLOCK
    span = window + BLOCK
    zero_rows = jnp.zeros((window, D), jnp.bfloat16)
    keys_padded = jnp.concatenate([zero_rows, key_rows])
    values_padded = jnp.concatenate([zero_rows, value_rows])

    def block_inputs(block_id):
        start_row = (block_id * BLOCK).astype(jnp.int32)
        query_heads = lax.dynamic_slice_in_dim(queries, start_row, BLOCK, 0).reshape(BLOCK, H, HD)
        key_block = lax.dynamic_slice_in_dim(keys_padded, start_row, span, 0).reshape(span, H, HD)
        value_block = lax.dynamic_slice_in_dim(values_padded, start_row, span, 0).reshape(span, H, HD)
        first_valid = jnp.maximum(window - start_row, 0).astype(jnp.int32)
        return start_row, query_heads, key_block, value_block, first_valid

    def forward_block(block_id):
        start_row, query_heads, key_block, value_block, first_valid = block_inputs(block_id)
        scores = block_scores(query_heads, key_block, alibi_slope, first_valid, window)
        log_norm = jax.nn.logsumexp(scores, axis=2)
        weights = jnp.exp(scores - log_norm[:, :, None]).astype(jnp.bfloat16)
        attn = jnp.einsum("hij,jhd->ihd", weights.astype(jnp.float32), value_block.astype(jnp.float32))
        return attn.astype(jnp.bfloat16).reshape(BLOCK, D), log_norm

    block_ids = jnp.arange(N_SEQ, dtype=jnp.int32)
    attn_blocks, norms = lax.map(forward_block, block_ids)
    attn_out = attn_blocks.reshape(TOKENS, D)

    ids_blocks = expert_ids.reshape(N_SEQ, BLOCK, 2)
    flat_ids = jnp.concatenate([ids_blocks[:, :, 0], ids_blocks[:, :, 1]], axis=1)
    position = slot_positions(flat_ids)
    is_kept = position < CAP
    block_index = lax.broadcasted_iota(jnp.int32, flat_ids.shape, 0)
    grad_blocks = out_grad.reshape(N_SEQ, BLOCK, D)
    gate_blocks = gate_values.reshape(N_SEQ, BLOCK, 2)
    token_flat = jnp.concatenate([attn_blocks, attn_blocks], axis=1)
    grad_flat = jnp.concatenate([gate_blocks[:, :, 0:1] * grad_blocks.astype(jnp.float32), gate_blocks[:, :, 1:2] * grad_blocks.astype(jnp.float32)], axis=1).astype(jnp.bfloat16)
    tokens_in = jnp.zeros((EXPERTS, N_SEQ, CAP, D), jnp.bfloat16).at[flat_ids, block_index, position].set(token_flat, mode="drop")
    grad_in = jnp.zeros((EXPERTS, N_SEQ, CAP, D), jnp.bfloat16).at[flat_ids, block_index, position].set(grad_flat, mode="drop")
    slot_rows = N_SEQ * CAP
    group_width = FF // N_EXP

    def expert_backward(operands):
        tokens, grad_rows, weight_in, weight_out = operands
        tokens = tokens.reshape(slot_rows, D)
        grad_rows = grad_rows.reshape(slot_rows, D)
        pre_act = jnp.dot(tokens, weight_in, preferred_element_type=jnp.float32)
        logistic = jax.nn.sigmoid(pre_act)
        hidden = (pre_act * logistic).astype(jnp.bfloat16)
        through_out = jnp.dot(grad_rows, weight_out.T, preferred_element_type=jnp.float32)
        hidden_grad = (through_out * logistic * (1.0 + pre_act * (1.0 - logistic))).astype(jnp.bfloat16)
        out_weight_grad = jnp.dot(hidden.T, grad_rows, preferred_element_type=jnp.float32).astype(jnp.bfloat16)
        in_weight_grad = jnp.dot(tokens.T, hidden_grad, preferred_element_type=jnp.float32).astype(jnp.bfloat16)
        grouped_grad = hidden_grad.reshape(slot_rows, N_EXP, group_width).astype(jnp.float32)
        grouped_weight = weight_in.reshape(D, N_EXP, group_width).astype(jnp.float32)
        partial_sums = jnp.einsum("rbf,dbf->brd", grouped_grad, grouped_weight).astype(jnp.bfloat16)
        back = jnp.sum(partial_sums.astype(jnp.float32), axis=0).astype(jnp.bfloat16)
        return in_weight_grad, out_weight_grad, back.reshape(N_SEQ, CAP, D)

    expert_in_grad, expert_out_grad, back_all = lax.map(expert_backward, (tokens_in, grad_in, expert_in, expert_out))
    picked = back_all[flat_ids, block_index, jnp.minimum(position, CAP - 1)].astype(jnp.float32)
    picked = jnp.where(is_kept[:, :, None], picked, 0.0)
    attn_grad_blocks = (grad_blocks.astype(jnp.float32) + picked[:, :BLOCK] + picked[:, BLOCK:]).astype(jnp.bfloat16)
    attn_grad = attn_grad_blocks.reshape(TOKENS, D)

    def backward_block(block_id, carry):
        query_total, key_total, value_total = carry
        block_id = jnp.asarray(block_id).astype(jnp.int32)
        start_row, query_heads, key_block, value_block, first_valid = block_inputs(block_id)
        attn_heads = lax.dynamic_slice_in_dim(attn_out, start_row, BLOCK, 0).reshape(BLOCK, H, HD).astype(jnp.float32)
        grad_heads = lax.dynamic_slice_in_dim(attn_grad, start_row, BLOCK, 0).reshape(BLOCK, H, HD).astype(jnp.float32)
        log_norm = lax.dynamic_index_in_dim(norms, block_id, 0, keepdims=False)
        scores = block_scores(query_heads, key_block, alibi_slope, first_valid, window)
        probs_full = jnp.exp(scores - log_norm[:, :, None])
        weights = probs_full.astype(jnp.bfloat16)
        row_delta = jnp.einsum("ihd,ihd->hi", grad_heads, attn_heads)
        dprob = jnp.einsum("ihd,jhd->hij", grad_heads, value_block.astype(jnp.float32))
        dscore = (probs_full * (dprob - row_delta[:, :, None])).astype(jnp.bfloat16).astype(jnp.float32)
        query_part = (jnp.einsum("hij,jhd->ihd", dscore, key_block.astype(jnp.float32)) * score_scale).astype(jnp.bfloat16)
        key_part = (jnp.einsum("hij,ihd->jhd", dscore, query_heads.astype(jnp.float32)) * score_scale).reshape(span, D)
        value_part = jnp.einsum("hij,ihd->jhd", weights.astype(jnp.float32), grad_heads).reshape(span, D)
        query_total = lax.dynamic_update_slice_in_dim(query_total, query_part.reshape(BLOCK, D), start_row, 0)
        key_old = lax.dynamic_slice_in_dim(key_total, start_row, span, 0)
        key_total = lax.dynamic_update_slice_in_dim(key_total, key_old + key_part, start_row, 0)
        value_old = lax.dynamic_slice_in_dim(value_total, start_row, span, 0)
        value_total = lax.dynamic_update_slice_in_dim(value_total, value_old + value_part, start_row, 0)
        return query_total, key_total, value_total

    start_carry = (jnp.zeros((TOKENS, D), jnp.bfloat16), jnp.zeros((window + TOKENS, D), jnp.float32), jnp.zeros((window + TOKENS, D), jnp.float32))
    query_grad, key_total, value_total = lax.fori_loop(0, N_SEQ, backward_block, start_carry)
    key_grad = key_total[window:].astype(jnp.bfloat16)
    value_grad = value_total[window:].astype(jnp.bfloat16)
    return (query_grad, key_grad, value_grad, expert_in_grad, expert_out_grad)
```

```python
import functools
import math

import jax
import jax.numpy as jnp
from jax import lax
from jax.experimental import pallas as pl
from jax.experimental.pallas import tpu as pltpu
from jax.sharding import PartitionSpec as P

HD = 128
WCH = 16
LOG2E = math.log2(math.e)
BF16 = jnp.bfloat16
F32 = jnp.float32
VMEM_LIMIT = 56 * 1024 * 1024


def on(pair, dims):
    return lax.dot_general(pair[0], pair[1], ((dims[0], dims[1]), ((), ())), preferred_element_type=F32)


def rows_by_rows(a, b):
    return on((a, b), ((1,), (1,)))


def cols_by_cols(a, b):
    return on((a, b), ((0,), (0,)))


def plain(a, b):
    return on((a, b), ((1,), (0,)))


def swap(block, axis, distance):
    if distance == 0:
        return block
    devices = range(lax.axis_size(axis))
    return lax.ppermute(block, axis, [(i, i ^ distance) for i in devices])


def local_call(body, out_shapes, scalars, arrays, scratch=(), flops=0, nbytes=0):
    smem = pl.BlockSpec(memory_space=pltpu.SMEM)
    vmem = pl.BlockSpec(memory_space=pltpu.VMEM)
    return pl.pallas_call(
        body,
        out_shape=[jax.ShapeDtypeStruct(shape, dtype) for shape, dtype in out_shapes],
        in_specs=[smem] * len(scalars) + [vmem] * len(arrays),
        out_specs=[vmem] * len(out_shapes),
        scratch_shapes=list(scratch),
        compiler_params=pltpu.CompilerParams(vmem_limit_bytes=VMEM_LIMIT),
        cost_estimate=pl.CostEstimate(flops=flops, bytes_accessed=nbytes, transcendentals=0),
    )(*scalars, *arrays)


def relative_slots(id_rows, place, experts, capacity, stride):
    flat = jnp.concatenate([id_rows[k : k + 1] for k in range(id_rows.shape[0])], axis=1)
    entries = flat.shape[1]
    flat = flat.astype(F32).astype(jnp.int32)
    lanes = max(experts, 8)
    one_hot = lax.broadcasted_iota(jnp.int32, (lanes, entries), 0) == flat
    one_hot = one_hot.astype(F32)
    earlier = lax.broadcasted_iota(jnp.int32, (entries, entries), 0) < lax.broadcasted_iota(
        jnp.int32, (entries, entries), 1
    )
    before = plain(one_hot.astype(BF16), earlier.astype(F32).astype(BF16))
    position = jnp.sum(before * one_hot, axis=0, keepdims=True).astype(jnp.int32)
    return jnp.where(position < capacity, (flat ^ place) * stride + position, -1)


def pack_body(sizes, idx, q, k, v, ids, *outs):
    G, R, BL = sizes
    g = idx[1]
    for d in range(G):
        cols = pl.ds(pl.multiple_of((g ^ d) * HD, HD), HD)
        outs[d][0:BL] = k[:, cols]
        outs[d][BL : 2 * BL] = v[:, cols]
        outs[d][2 * BL : 3 * BL] = q[:, cols]
        outs[d][3 * BL : 3 * BL + 16] = ids[...]


def grads_body(sizes, idx, og, gates, ids, *outs):
    G, R, BL, cap, stride = sizes
    n = G * R
    s, g = idx[0], idx[1]
    slots = relative_slots(ids[0 : 2 * BL // 128], s, n, cap, stride)
    routing = lax.broadcasted_iota(jnp.int32, (n * stride, 2 * BL), 0) == slots
    block = og[...].astype(F32)
    scaled = jnp.concatenate([(gates[:, j : j + 1] * block).astype(BF16) for j in range(2)], axis=0)
    routed = plain(routing.astype(F32).astype(BF16), scaled).astype(BF16)
    for d in range(n):
        outs[d][...] = routed[d * stride : (d + 1) * stride]
    for d in range(G):
        outs[n + d][...] = og[:, pl.ds(pl.multiple_of((g ^ d) * HD, HD), HD)]


def forward_body(sizes, idx, slopes, *refs):
    G, R, BL, cap, stride = sizes
    n = G * R
    total = n * BL
    s, g, r = idx[0], idx[1], idx[2]
    own, refs = refs[:G], refs[G:]
    others, refs = refs[: G * (R - 1)], refs[G * (R - 1) :]
    probs, refs = refs[:G], refs[G:]
    sent, refs = refs[:n], refs[n:]
    attn, routing, keys, values, queries, ids = refs
    for d in range(G):
        i = g ^ d
        queries[pl.ds(pl.multiple_of(i * BL, BL), BL)] = own[d][2 * BL : 3 * BL]
        ids[pl.ds(i, 1)] = own[d][3 * BL : 3 * BL + 16].astype(F32)[None]
        for dr in range(R):
            piece = own[d] if dr == 0 else others[(dr - 1) * G + d]
            rows = pl.ds(pl.multiple_of((i * R + (r ^ dr)) * BL, BL), BL)
            keys[rows] = piece[0:BL]
            values[rows] = piece[BL : 2 * BL]
    slope = slopes[g]
    span = R * BL
    for i in range(G):
        slots = relative_slots(ids[i][0 : 2 * BL // 128], s, n, cap, stride)
        slot_rows = lax.broadcasted_iota(jnp.int32, (n * stride, BL), 0)
        chosen = (slot_rows == slots[:, :BL]) | (slot_rows == slots[:, BL:])
        chosen = chosen.astype(F32).astype(BF16)
        routing[i] = chosen
        N = (i + 1) * span
        scores = rows_by_rows(queries[i * BL : (i + 1) * BL], keys[0:N])
        col = lax.broadcasted_iota(jnp.int32, (1, N), 1)
        bias = (col - N).astype(F32) * (slope * LOG2E)
        scores = scores * (HD**-0.5 * LOG2E) + bias
        if total > WCH * BL:
            distance = (
                lax.broadcasted_iota(jnp.int32, (BL, N), 0) + (i * R + r) * BL - lax.broadcasted_iota(jnp.int32, (BL, N), 1)
            )
            scores = jnp.where((distance >= 0) & (distance < WCH * BL), scores, -jnp.inf)
        else:
            ahead = lax.broadcasted_iota(jnp.int32, (BL, span), 1) - lax.broadcasted_iota(jnp.int32, (BL, span), 0)
            last = jnp.where(ahead <= r * BL, scores[:, N - span :], -jnp.inf)
            scores = last if i == 0 else jnp.concatenate([scores[:, : N - span], last], axis=1)
        top = jnp.max(scores, axis=1, keepdims=True)
        grown = jnp.exp2(scores - top)
        norm = jnp.sum(grown, axis=1, keepdims=True)
        weights = (grown * (1.0 / norm)).astype(BF16)
        probs[i][...] = weights
        out = plain(weights, values[0:N]).astype(BF16)
        attn[i * BL : (i + 1) * BL] = out
        routed = plain(chosen, out).astype(BF16)
        for d in range(n):
            sent[d][i * stride : (i + 1) * stride] = routed[d * stride : (d + 1) * stride]


def backward_body(sizes, idx, *refs):
    G, R, BL, cap, stride = sizes
    n = G * R
    g, r = idx[1], idx[2]
    back, refs = refs[:n], refs[n:]
    upper, refs = refs[:G], refs[G:]
    probs, refs = refs[:G], refs[G:]
    attn, routing, keys, values, queries = refs[:5]
    refs = refs[5:]
    query_out, refs = refs[:G], refs[G:]
    pair_out, refs = refs[: G * R], refs[G * R :]
    upper_rows, query_rows, key_sum, value_sum = refs
    scale = HD**-0.5
    for d in range(G):
        upper_rows[pl.ds(pl.multiple_of((g ^ d) * BL, BL), BL)] = upper[d][...]
    for i in reversed(range(G)):
        N = (i + 1) * R * BL
        mine = slice(i * BL, (i + 1) * BL)
        rows = jnp.concatenate([back[d][i * stride : (i + 1) * stride] for d in range(n)], axis=0)
        picked = cols_by_cols(routing[i], rows)
        grad = (upper_rows[mine].astype(F32) + picked).astype(BF16)
        delta = jnp.sum(grad.astype(F32) * attn[mine].astype(F32), axis=1, keepdims=True)
        weights = probs[i][...]
        dprob = rows_by_rows(grad, values[0:N])
        dscore = (weights.astype(F32) * (dprob - delta)).astype(BF16)
        query_rows[mine] = (plain(dscore, keys[0:N]) * scale).astype(BF16)
        key_part = cols_by_cols(dscore, queries[mine]) * scale
        value_part = cols_by_cols(weights, grad)
        if i == G - 1:
            key_sum[...] = key_part
            value_sum[...] = value_part
        else:
            key_sum[0:N] += key_part
            value_sum[0:N] += value_part
    for d in range(G):
        i = g ^ d
        query_out[d][...] = query_rows[pl.ds(pl.multiple_of(i * BL, BL), BL)]
        for dr in range(R):
            rows = pl.ds(pl.multiple_of((i * R + (r ^ dr)) * BL, BL), BL)
            pair_out[dr * G + d][0:BL] = key_sum[rows].astype(BF16)
            pair_out[dr * G + d][BL : 2 * BL] = value_sum[rows].astype(BF16)


def unpack_body(sizes, idx, *refs):
    G, R, BL = sizes
    g = idx[1]
    query_in, pair_in, outs = refs[:G], refs[G : 2 * G], refs[2 * G :]
    for d in range(G):
        cols = pl.ds(pl.multiple_of((g ^ d) * HD, HD), HD)
        outs[0][:, cols] = query_in[d][...]
        outs[1][:, cols] = pair_in[d][0:BL]
        outs[2][:, cols] = pair_in[d][BL : 2 * BL]


def gather_tokens_body(sizes, idx, *refs):
    G, R, rows = sizes
    g = idx[1]
    out = refs[-1]
    for dg in range(G):
        cols = pl.ds(pl.multiple_of((g ^ dg) * HD, HD), HD)
        for dr in range(R):
            out[dr * rows : (dr + 1) * rows, cols] = refs[dg * R + dr][...]


def gather_grads_body(sizes, idx, *refs):
    G, R, stride = sizes
    g = idx[1]
    out = refs[-1]
    for dg in range(G):
        for dr in range(R):
            at = pl.multiple_of((dr * G + (g ^ dg)) * stride, 16)
            out[pl.ds(at, stride)] = refs[dg * R + dr][...]


def through_body(idx, *refs):
    shards, weight, out = refs[:-2], refs[-2], refs[-1]
    width = shards[0].shape[1]
    total = None
    for k, shard in enumerate(shards):
        cols = pl.ds(pl.multiple_of((idx[3] ^ k) * width, 128), width)
        part = rows_by_rows(shard[...], weight[:, cols])
        total = part if total is None else total + part
    out[...] = total


def pre_body(first, start, idx, *refs):
    if start is None:
        shards, weight, out = refs[:-2], refs[-2], refs[-1]
        total = None
    else:
        shards, weight, begun, through, hidden, hidden_grad = refs[:-5], refs[-5], refs[-4], refs[-3], refs[-2], refs[-1]
        total = begun[...]
    width = shards[0].shape[1]
    for k, shard in enumerate(shards):
        rows = pl.ds(pl.multiple_of((idx[3] ^ (first + k)) * width, 128), width)
        part = plain(shard[...], weight[rows, :])
        total = part if total is None else total + part
    if start is None:
        out[...] = total
    else:
        logistic = 1.0 / (1.0 + jnp.exp(-total))
        hidden[...] = (total * logistic).astype(BF16)
        hidden_grad[...] = (through[...] * logistic * (1.0 + total * (1.0 - logistic))).astype(BF16)


def back_body(shards, idx, grad, weight, out):
    width = out.shape[2]
    for at, k in enumerate(shards):
        rows = pl.ds(pl.multiple_of((idx[3] ^ k) * width, 128), width)
        out[at] = rows_by_rows(grad[...], weight[rows, :]).astype(BF16)


def out_weight_body(idx, hidden, *refs):
    out = refs[-1]
    width = refs[0].shape[1]
    for k, shard in enumerate(refs[:-1]):
        cols = pl.ds(pl.multiple_of((idx[3] ^ k) * width, 128), width)
        out[:, cols] = cols_by_cols(hidden[...], shard[...]).astype(BF16)


def in_weight_body(idx, grad, *refs):
    out = refs[-1]
    width = refs[0].shape[1]
    for k, shard in enumerate(refs[:-1]):
        rows = pl.ds(pl.multiple_of((idx[3] ^ k) * width, 128), width)
        out[rows, :] = cols_by_cols(shard[...], grad[...]).astype(BF16)


def gather_exp(block, size):
    shards = [block]
    distance = size // 2
    by_place = {0: block}
    while distance:
        for place in list(by_place):
            by_place[place ^ distance] = swap(by_place[place], "exp", distance)
        distance //= 2
    shards = [by_place[k] for k in range(size)]
    return shards


def per_device(
    queries,
    key_rows,
    value_rows,
    out_grad,
    expert_ids,
    gate_values,
    alibi_slope,
    expert_in,
    expert_out,
):
    BL, features = queries.shape
    G = features // HD
    n = lax.axis_size("seq")
    E = lax.axis_size("exp")
    R = n // G
    cap = 5 * BL // (2 * n)
    stride = -(-cap // 16) * 16
    rows = n * stride
    FFL = expert_in.shape[2]
    L = n * BL
    seq_index = lax.axis_index("seq")
    idx = jnp.stack([seq_index, seq_index // R, seq_index % R, lax.axis_index("exp")]).astype(jnp.int32)
    weight_in = expert_in[0]
    weight_out = expert_out[0]

    id_rows = expert_ids.T.reshape(2 * BL // 128, 128).astype(BF16)
    id_rows = jnp.pad(id_rows, ((0, 16 - 2 * BL // 128), (0, 0)))
    payload = local_call(
        functools.partial(pack_body, (G, R, BL)),
        [((3 * BL + 16, HD), BF16)] * G,
        [idx],
        [queries, key_rows, value_rows, id_rows],
        nbytes=6 * BL * features * 2,
    )
    own = [swap(payload[d], "seq", d * R) for d in range(G)]
    others = [swap(own[d][: 2 * BL], "seq", dr) for dr in range(1, R) for d in range(G)]

    sent = local_call(
        functools.partial(grads_body, (G, R, BL, cap, stride)),
        [((stride, features), BF16)] * n + [((BL, HD), BF16)] * G,
        [idx],
        [out_grad, gate_values, id_rows],
        flops=2 * rows * 2 * BL * features,
        nbytes=3 * BL * features * 2,
    )
    grad_pieces = [swap(sent[d], "seq", d) for d in range(n)]
    upper = [swap(sent[n + d], "seq", d * R) for d in range(G)]

    shapes = [((BL, (i + 1) * R * BL), BF16) for i in range(G)]
    shapes += [((G * stride, HD), BF16)] * n
    shapes += [((G * BL, HD), BF16), ((G, rows, BL), BF16), ((L, HD), BF16), ((L, HD), BF16), ((G * BL, HD), BF16)]
    made = local_call(
        functools.partial(forward_body, (G, R, BL, cap, stride)),
        shapes,
        [idx, alibi_slope],
        own + others,
        scratch=[pltpu.VMEM((G, 16, 128), F32)],
        flops=4 * G * BL * L * HD,
        nbytes=10 * 1024 * 1024,
    )
    probs, made = made[:G], made[G:]
    token_sent, made = made[:n], made[n:]
    attn, routing, keys, values, query_rows = made

    grads = local_call(
        functools.partial(gather_grads_body, (G, R, stride)),
        [((rows, features), BF16)],
        [idx],
        grad_pieces,
        nbytes=rows * features * 4,
    )[0]
    grad_shards = gather_exp(grads, E)
    through = local_call(
        through_body,
        [((rows, FFL), F32)],
        [idx],
        grad_shards + [weight_out],
        flops=2 * rows * FFL * features * E,
        nbytes=10 * 1024 * 1024,
    )[0]

    token_pieces = [swap(token_sent[d], "seq", d) for d in range(n)]
    tokens = local_call(
        functools.partial(gather_tokens_body, (G, R, G * stride)),
        [((rows, features), BF16)],
        [idx],
        token_pieces,
        nbytes=rows * features * 4,
    )[0]
    token_shards = gather_exp(tokens, E)
    half = E // 2
    begun = local_call(
        functools.partial(pre_body, 0, None),
        [((rows, FFL), F32)],
        [idx],
        token_shards[:half] + [weight_in],
        flops=2 * rows * FFL * features * half,
        nbytes=8 * 1024 * 1024,
    )[0]
    hidden, hidden_grad = local_call(
        functools.partial(pre_body, half, True),
        [((rows, FFL), BF16)] * 2,
        [idx],
        token_shards[half:] + [weight_in, begun, through],
        flops=2 * rows * FFL * features * half,
        nbytes=8 * 1024 * 1024,
    )

    def back_parts(shards):
        return local_call(
            functools.partial(back_body, shards),
            [((len(shards), rows, features), BF16)],
            [idx],
            [hidden_grad, weight_in],
            flops=2 * rows * FFL * features * len(shards),
            nbytes=8 * 1024 * 1024,
        )[0]

    odd = list(range(1, E, 2))
    even = list(range(0, E, 2))
    held = back_parts(odd)
    moved = swap(held, "exp", 1)
    kept = back_parts(even)
    held = [(kept[k].astype(F32) + moved[k].astype(F32)) for k in range(E // 2)]
    distance = E // 2
    while distance > 1:
        count = len(held) // 2
        moved = [swap(held[count + k].astype(BF16), "exp", distance) for k in range(count)]
        held = [held[k] + moved[k].astype(F32) for k in range(count)]
        distance //= 2
    back = held[0].astype(BF16)

    g = idx[1]
    back_view = back.reshape(R, G * stride, features)
    back_sent = [
        lax.dynamic_slice_in_dim(back_view[d % R], (g ^ (d // R)) * HD, HD, axis=1) for d in range(n)
    ]
    returned = [swap(back_sent[d], "seq", d) for d in range(n)]

    out_weight_grad = local_call(
        out_weight_body,
        [((FFL, features * E), BF16)],
        [idx],
        [hidden] + grad_shards,
        flops=2 * rows * FFL * features * E,
        nbytes=10 * 1024 * 1024,
    )[0]
    in_weight_grad = local_call(
        in_weight_body,
        [((features * E, FFL), BF16)],
        [idx],
        [hidden_grad] + token_shards,
        flops=2 * rows * FFL * features * E,
        nbytes=10 * 1024 * 1024,
    )[0]

    made = local_call(
        functools.partial(backward_body, (G, R, BL, cap, stride)),
        [((BL, HD), BF16)] * G + [((2 * BL, HD), BF16)] * (G * R),
        [idx],
        returned + upper + list(probs) + [attn, routing, keys, values, query_rows],
        scratch=[
            pltpu.VMEM((G * BL, HD), BF16),
            pltpu.VMEM((G * BL, HD), BF16),
            pltpu.VMEM((L, HD), F32),
            pltpu.VMEM((L, HD), F32),
        ],
        flops=8 * G * BL * L * HD,
        nbytes=10 * 1024 * 1024,
    )
    query_pieces, pair_pieces = made[:G], made[G:]
    query_home = [swap(query_pieces[d], "seq", d * R) for d in range(G)]
    pair_home = []
    for d in range(G):
        total = pair_pieces[d].astype(F32)
        for dr in range(1, R):
            total = total + swap(pair_pieces[dr * G + d], "seq", dr).astype(F32)
        pair_home.append(swap(total.astype(BF16), "seq", d * R))
    query_grad, key_grad, value_grad = local_call(
        functools.partial(unpack_body, (G, R, BL)),
        [((BL, features), BF16)] * 3,
        [idx],
        query_home + pair_home,
        nbytes=6 * BL * features * 2,
    )
    return query_grad, key_grad, value_grad, in_weight_grad[None], out_weight_grad[None]


def solution(mesh):
    return jax.shard_map(
        per_device,
        mesh=mesh,
        in_specs=(
            P("seq", "exp"),
            P("seq", "exp"),
            P("seq", "exp"),
            P("seq", "exp"),
            P("seq", None),
            P("seq", None),
            P("exp"),
            P("seq", None, "exp"),
            P("seq", "exp", None),
        ),
        out_specs=(
            P("seq", "exp"),
            P("seq", "exp"),
            P("seq", "exp"),
            P("seq", None, "exp"),
            P("seq", "exp", None),
        ),
        check_vma=False,
    )
```

```python
import functools
import math

import jax
import jax.numpy as jnp
from jax import lax
from jax.experimental import pallas as pl
from jax.experimental.pallas import tpu as pltpu
from jax.sharding import PartitionSpec as P

HD = 128
WCH = 16
LOG2E = math.log2(math.e)
BF16 = jnp.bfloat16
F32 = jnp.float32
MIB = 1024 * 1024
VMEM_LIMIT = 14 * MIB


def on(pair, dims):
    return lax.dot_general(pair[0], pair[1], ((dims[0], dims[1]), ((), ())), preferred_element_type=F32)


def rows_by_rows(a, b):
    return on((a, b), ((1,), (1,)))


def cols_by_cols(a, b):
    return on((a, b), ((0,), (0,)))


def plain(a, b):
    return on((a, b), ((1,), (0,)))


def swap(block, axis, distance):
    if distance == 0:
        return block
    devices = range(lax.axis_size(axis))
    return lax.ppermute(block, axis, [(i, i ^ distance) for i in devices])


def local_call(body, out_shapes, arrays, scalars=(), after=(), far=(), into=(), aliases=None, scratch=(), flops=0, nbytes=0, limit=VMEM_LIMIT):
    smem = pl.BlockSpec(memory_space=pltpu.SMEM)
    vmem = pl.BlockSpec(memory_space=pltpu.VMEM)
    anywhere = pl.BlockSpec(memory_space=pl.ANY)
    hbm = pl.BlockSpec(memory_space=pltpu.HBM)
    lead = len(scalars)
    grid = (1,) if any(isinstance(x, tuple) for x in arrays) else ()
    specs = [pl.BlockSpec(x[1], lambda j, at=x[2]: at) if isinstance(x, tuple) else vmem for x in arrays] + [hbm] * len(into)
    arrays = [x[0] if isinstance(x, tuple) else x for x in arrays]

    def kernel(*refs):
        body(*refs[:lead], *refs[lead + len(after) :])

    return pl.pallas_call(
        kernel,
        out_shape=[jax.ShapeDtypeStruct(x[0], x[1]) for x in out_shapes],
        grid=grid,
        in_specs=[smem] * lead + [anywhere] * len(after) + [hbm] * len(far) + specs,
        out_specs=[pl.BlockSpec(memory_space=x[2]) if len(x) > 2 else vmem for x in out_shapes],
        scratch_shapes=list(scratch),
        input_output_aliases=aliases or {},
        compiler_params=pltpu.CompilerParams(vmem_limit_bytes=limit),
        cost_estimate=pl.CostEstimate(flops=flops, bytes_accessed=nbytes, transcendentals=0),
    )(*scalars, *after, *far, *arrays, *into)


def hold(arrays, after):
    def body(*refs):
        pass

    anywhere = pl.BlockSpec(memory_space=pl.ANY)
    lead = len(after)
    return list(
        pl.pallas_call(
            body,
            out_shape=[jax.ShapeDtypeStruct(x.shape, x.dtype) for x in arrays],
            in_specs=[anywhere] * (lead + len(arrays)),
            out_specs=[anywhere] * len(arrays),
            input_output_aliases={lead + at: at for at in range(len(arrays))},
            compiler_params=pltpu.CompilerParams(vmem_limit_bytes=MIB),
        )(*after, *arrays)
    )


def grid_call(body, steps, exp_index, ins, outs, after=(), flops=0, nbytes=0, limit=VMEM_LIMIT):
    anywhere = pl.BlockSpec(memory_space=pl.ANY)

    def kernel(place, *refs):
        body(place[0], *refs[len(after) :])

    return pl.pallas_call(
        kernel,
        out_shape=[jax.ShapeDtypeStruct(shape, dtype) for shape, dtype, _, _ in outs],
        grid_spec=pltpu.PrefetchScalarGridSpec(
            num_scalar_prefetch=1,
            grid=(steps,),
            in_specs=[anywhere] * len(after) + [pl.BlockSpec(block, index) for _, block, index in ins],
            out_specs=[pl.BlockSpec(block, index) for _, _, block, index in outs],
        ),
        compiler_params=pltpu.CompilerParams(vmem_limit_bytes=limit),
        cost_estimate=pl.CostEstimate(flops=flops, bytes_accessed=nbytes, transcendentals=0),
    )(exp_index, *after, *[array for array, _, _ in ins])


def attention_limit(block_len, total):
    return min(60 * MIB, 4 * MIB + 6 * block_len * total * 4)


def id_rows_of(ids):
    return [ids[j : j + 1, at : at + 128].astype(F32) for j in range(2) for at in range(0, ids.shape[1], 128)]


def relative_slots(id_rows, place, experts, capacity, stride):
    flat = jnp.concatenate(id_rows, axis=1).astype(jnp.int32)
    entries = flat.shape[1]
    lanes = max(experts, 8)
    one_hot = lax.broadcasted_iota(jnp.int32, (lanes, entries), 0) == flat
    one_hot = one_hot.astype(F32)
    earlier = lax.broadcasted_iota(jnp.int32, (entries, entries), 0) < lax.broadcasted_iota(
        jnp.int32, (entries, entries), 1
    )
    before = plain(one_hot.astype(BF16), earlier.astype(F32).astype(BF16))
    position = jnp.sum(before * one_hot, axis=0, keepdims=True).astype(jnp.int32)
    return jnp.where(position < capacity, (flat ^ place) * stride + position, -1)


def pack_body(sizes, q, k, v, og, ids, gates, *refs):
    G, R, BL = sizes[:3]
    outs, sent, place, held, sems = refs[:G], refs[G : G + R], *refs[G + R :]
    g = lax.axis_index("seq") // R
    place[0] = lax.axis_index("exp")

    moves = [pltpu.make_async_copy(source, held.at[at], sems.at[at]) for at, source in enumerate((k, v, q, og))]
    for move in moves:
        move.start()
    rows = id_rows_of(ids)
    rows.append(jnp.zeros((16 - len(rows), 128), F32))
    rows = jnp.concatenate(rows, axis=0).astype(BF16)
    for d in range(G):
        outs[d][3 * BL : 3 * BL + 16] = rows
    for at, move in enumerate(moves[:3]):
        move.wait()
        for d in range(G):
            cols = pl.ds(pl.multiple_of((g ^ d) * HD, HD), HD)
            outs[d][at * BL : (at + 1) * BL] = held[at, :, cols]
    moves[3].wait()
    route_grads(sizes, held[3], gates, ids, sent)


def upper_body(sizes, og, *refs):
    G, R, BL = sizes
    outs, sems = refs[:G], refs[G]
    g = lax.axis_index("seq") // R
    moves = []
    for d in range(G):
        cols = pl.ds(pl.multiple_of((g ^ d) * HD, HD), HD)
        moves.append(pltpu.make_async_copy(og.at[:, cols], outs[d], sems.at[d]))
    for move in moves:
        move.start()
    for move in moves:
        move.wait()


def route_grads(sizes, block, gates, ids, outs):
    G, R, BL, cap, stride = sizes
    n = G * R
    slots = relative_slots(id_rows_of(ids), lax.axis_index("seq"), n, cap, stride)
    routing = lax.broadcasted_iota(jnp.int32, (n * stride, 2 * BL), 0) == slots
    diagonal = lax.broadcasted_iota(jnp.int32, (BL, BL), 0) == lax.broadcasted_iota(jnp.int32, (BL, BL), 1)
    block = block.astype(F32)
    scaled = []
    for j in range(2):
        gate = jnp.sum(jnp.where(diagonal, gates[j : j + 1], 0.0), axis=1, keepdims=True)
        scaled.append((gate * block).astype(BF16))
    routed = plain(routing.astype(F32).astype(BF16), jnp.concatenate(scaled, axis=0)).astype(BF16)
    for dg in range(G):
        for dr in range(R):
            d = dg * R + dr
            outs[dr][dg * stride : (dg + 1) * stride] = routed[d * stride : (d + 1) * stride]


def routing_body(sizes, *refs):
    G, R, BL, cap, stride = sizes
    n = G * R
    s = lax.axis_index("seq")
    own, out = refs[:G], refs[G]
    for d in range(G):
        rows = own[d][...].astype(F32)
        slots = relative_slots([rows[k : k + 1] for k in range(2 * BL // 128)], s, n, cap, stride)
        slot_rows = lax.broadcasted_iota(jnp.int32, (n * stride, BL), 0)
        chosen = (slot_rows == slots[:, :BL]) | (slot_rows == slots[:, BL:])
        out[pl.ds((s // R) ^ d, 1)] = chosen.astype(F32).astype(BF16)[None]


def pair_groups(G):
    return [members for members in ([0], [1], list(range(2, G))) if members and members[-1] < G]


def forward_body(sizes, slopes, *refs):
    G, R, BL, cap, stride = sizes
    n = G * R
    total = n * BL
    s = lax.axis_index("seq")
    g, r = s // R, s % R
    own, refs = refs[:G], refs[G:]
    groups = pair_groups(G)
    others, refs = refs[: len(groups) * (R - 1)], refs[len(groups) * (R - 1) :]
    far, refs = refs[: G + 4], refs[G + 4 :]
    attn_out, refs = refs[0], refs[1:]
    near, sems = refs[: G + 4], refs[G + 4]
    probs = near[:G]
    attn, keys, values, queries = near[G:]

    def kept(at):
        return pltpu.make_async_copy(near[at], far[at], sems.at[at])

    for d in range(G):
        i = g ^ d
        queries[pl.ds(pl.multiple_of(i * BL, BL), BL)] = own[d][2 * BL : 3 * BL]
        for dr in range(R):
            piece, at = own[d], 0
            if dr:
                group = next(k for k, members in enumerate(groups) if d in members)
                piece = others[(dr - 1) * len(groups) + group]
                at = groups[group].index(d) * 2 * BL
            rows = pl.ds(pl.multiple_of((i * R + (r ^ dr)) * BL, BL), BL)
            keys[rows] = piece[at : at + BL]
            values[rows] = piece[at + BL : at + 2 * BL]
    for at in range(G + 1, G + 4):
        kept(at).start()
    slope = slopes[g]
    span = R * BL
    for i in range(G):
        N = (i + 1) * span
        scores = rows_by_rows(queries[i * BL : (i + 1) * BL], keys[0:N])
        col = lax.broadcasted_iota(jnp.int32, (1, N), 1)
        bias = (col - N).astype(F32) * (slope * LOG2E)
        scores = scores * (HD**-0.5 * LOG2E) + bias
        if total > WCH * BL:
            distance = (
                lax.broadcasted_iota(jnp.int32, (BL, N), 0) + (i * R + r) * BL - lax.broadcasted_iota(jnp.int32, (BL, N), 1)
            )
            scores = jnp.where((distance >= 0) & (distance < WCH * BL), scores, -jnp.inf)
        else:
            ahead = lax.broadcasted_iota(jnp.int32, (BL, span), 1) - lax.broadcasted_iota(jnp.int32, (BL, span), 0)
            last = jnp.where(ahead <= r * BL, scores[:, N - span :], -jnp.inf)
            scores = last if i == 0 else jnp.concatenate([scores[:, : N - span], last], axis=1)
        top = jnp.max(scores, axis=1, keepdims=True)
        grown = jnp.exp2(scores - top)
        norm = jnp.sum(grown, axis=1, keepdims=True)
        weights = (grown * (1.0 / norm)).astype(BF16)
        probs[i][...] = weights
        kept(i).start()
        out = plain(weights, values[0:N]).astype(BF16)
        attn[i * BL : (i + 1) * BL] = out
        attn_out[i * BL : (i + 1) * BL] = out
    kept(G).start()
    for at in range(G + 4):
        kept(at).wait()


def dispatch_body(sizes, attn, routing, *sent):
    G, R, BL, cap, stride = sizes
    for i in range(G):
        routed = plain(routing[i], attn[i * BL : (i + 1) * BL]).astype(BF16)
        for dg in range(G):
            for dr in range(R):
                d = dg * R + dr
                at = (dr * G + i) * stride
                sent[dg][at : at + stride] = routed[d * stride : (d + 1) * stride]


def value_body(sizes, *refs):
    G, R, BL, cap, stride = sizes
    n = G * R
    s = lax.axis_index("seq")
    g, r = s // R, s % R
    back, refs = refs[:G], refs[G:]
    upper, refs = refs[:G], refs[G:]
    probs, refs = refs[:G], refs[G:]
    routing, attn_grad, refs = refs[0], refs[1], refs[2:]
    outs, total, upper_rows = refs[:R], refs[R], refs[R + 1]
    for d in range(G):
        upper_rows[pl.ds(pl.multiple_of((g ^ d) * BL, BL), BL)] = upper[d][...]
    for i in reversed(range(G)):
        N = (i + 1) * R * BL
        mine = slice(i * BL, (i + 1) * BL)
        starts = [(dr * G + i) * stride for dr in range(R)]
        rows = jnp.concatenate([back[dg][at : at + stride] for dg in range(G) for at in starts], axis=0)
        picked = cols_by_cols(routing[i], rows)
        grad = (upper_rows[mine].astype(F32) + picked).astype(BF16)
        attn_grad[mine] = grad
        part = cols_by_cols(probs[i][...], grad)
        if i == G - 1:
            total[...] = part
        else:
            total[0:N] += part
    spread(sizes, total, outs)


def spread(sizes, total, outs):
    G, R, BL = sizes[:3]
    s = lax.axis_index("seq")
    g, r = s // R, s % R
    for d in range(G):
        for dr in range(R):
            rows = pl.ds(pl.multiple_of(((g ^ d) * R + (r ^ dr)) * BL, BL), BL)
            outs[dr][d * BL : (d + 1) * BL] = total[rows].astype(BF16)


def score_body(sizes, *refs):
    G, R, BL = sizes[:3]
    s = lax.axis_index("seq")
    g = s // R
    probs, refs = refs[:G], refs[G:]
    attn_grad, attn, keys, values, queries = refs[:5]
    refs = refs[5:]
    query_out, refs = refs[:G], refs[G:]
    outs, query_rows, total = refs[:R], refs[R], refs[R + 1]
    scale = HD**-0.5
    for i in reversed(range(G)):
        N = (i + 1) * R * BL
        mine = slice(i * BL, (i + 1) * BL)
        grad = attn_grad[mine]
        delta = jnp.sum(grad.astype(F32) * attn[mine].astype(F32), axis=1, keepdims=True)
        dprob = rows_by_rows(grad, values[0:N])
        dscore = (probs[i][...].astype(F32) * (dprob - delta)).astype(BF16)
        query_rows[mine] = (plain(dscore, keys[0:N]) * scale).astype(BF16)
        part = cols_by_cols(dscore, queries[mine]) * scale
        if i == G - 1:
            total[...] = part
        else:
            total[0:N] += part
    for d in range(G):
        query_out[d][...] = query_rows[pl.ds(pl.multiple_of((g ^ d) * BL, BL), BL)]
    spread(sizes, total, outs)


def unpack_body(sizes, *refs):
    G, R, BL = sizes
    g = lax.axis_index("seq") // R
    pieces, outs = refs[: 3 * G], refs[3 * G :]
    for at in range(3):
        for d in range(G):
            cols = pl.ds(pl.multiple_of((g ^ d) * HD, HD), HD)
            outs[at][:, cols] = pieces[at * G + d][...]


def turn_tokens_body(sizes, *refs):
    G, R, count = sizes
    g = lax.axis_index("seq") // R
    for dg in range(G):
        cols = pl.ds(pl.multiple_of((g ^ dg) * HD, HD), HD)
        for dr in range(R):
            refs[G + dr][:, cols] = refs[dg][dr * count : (dr + 1) * count]


def column_body(sizes, *refs):
    G, R, stride = sizes
    for dg in range(G):
        for dr in range(R):
            refs[R + dg][dr * stride : (dr + 1) * stride] = refs[dr][dg * stride : (dg + 1) * stride]


def turn_grads_body(sizes, *refs):
    G, R, stride = sizes
    g = lax.axis_index("seq") // R
    for dg in range(G):
        for dr in range(R):
            at = pl.ds(pl.multiple_of((dr * G + (g ^ dg)) * stride, 16), stride)
            refs[-1][at] = refs[dg][dr * stride : (dr + 1) * stride]


def turn_back_body(sizes, near, arrived, *refs):
    G, R, count = sizes
    g = lax.axis_index("seq") // R
    moved, outs = refs[: R - 1], refs[R - 1 :]
    for dg in range(G):
        cols = pl.ds(pl.multiple_of((g ^ dg) * HD, HD), HD)
        outs[dg][0:count] = (near[0:count, cols] + arrived[0:count, cols].astype(F32)).astype(BF16)
        for dr in range(1, R):
            outs[dg][dr * count : (dr + 1) * count] = moved[dr - 1][:, cols]


def keep_moves(parts, first, shards, full, sems):
    place = lax.axis_index("exp")
    rows, width = shards[0].shape
    moves = []
    for at, shard in enumerate(shards):
        k, h = first + at // parts, at % parts
        cols = pl.ds(pl.multiple_of((place ^ k) * width, 128), width)
        moves.append(pltpu.make_async_copy(shard, full.at[pl.ds(h * rows, rows), cols], sems.at[at]))
    return moves


def through_body(parts, weight, *refs):
    shards, out, full, held, sems, own_sems = refs[:-5], *refs[-5:]
    place = lax.axis_index("exp")
    rows, width = shards[0].shape
    steps = sems.shape[0]
    kept = keep_moves(parts, 0, shards, full, own_sems)
    tall = weight.shape[0] // steps

    def fetch(c):
        mine = pl.ds(c * tall, tall)
        return pltpu.make_async_copy(weight.at[mine], held.at[mine], sems.at[c])

    for c in range(steps):
        fetch(c).start()
    for move in kept:
        move.start()
    for c in range(steps):
        fetch(c).wait()
        for h in range(parts):
            total = None
            for k in range(len(shards) // parts):
                cols = pl.ds(pl.multiple_of((place ^ k) * width, 128), width)
                part = rows_by_rows(shards[k * parts + h][...], held[c * tall : (c + 1) * tall, cols])
                total = part if total is None else total + part
            out[h * rows : (h + 1) * rows, c * tall : (c + 1) * tall] = total
    for move in kept:
        move.wait()


def pre_body(parts, first, weight, *refs):
    held, sems, own_sems = refs[-3:]
    if first:
        shards, begun, through, full, hidden, hidden_grad = refs[:-9], *refs[-9:-7], *refs[-6:-3]
    else:
        shards, out, full = refs[:-5], *refs[-5:-3]
    kept = keep_moves(parts, first, shards, full, own_sems)
    place = lax.axis_index("exp")
    rows, width = shards[0].shape
    count, steps = sems.shape
    wide = weight.shape[1] // steps

    def fetch(k, c):
        source = weight.at[pl.ds(pl.multiple_of((place ^ (first + k)) * width, 128), width), pl.ds(c * wide, wide)]
        return pltpu.make_async_copy(source, held.at[c, pl.ds(k * width, width)], sems.at[k, c])

    for c in range(steps):
        for k in range(count):
            fetch(k, c).start()
    for move in kept:
        move.start()
    for c in range(steps):
        cols = slice(c * wide, (c + 1) * wide)
        for k in range(count):
            fetch(k, c).wait()
        for h in range(parts):
            mine = slice(h * rows, (h + 1) * rows)
            total = begun[mine, cols] if first else None
            for k in range(count):
                part = plain(shards[k * parts + h][...], held[c, k * width : (k + 1) * width])
                total = part if total is None else total + part
            if not first:
                out[mine, cols] = total
            else:
                logistic = 1.0 / (1.0 + jnp.exp(-total))
                hidden[mine, cols] = (total * logistic).astype(BF16)
                grad = through[mine, cols] * logistic * (1.0 + total * (1.0 - logistic))
                hidden_grad[mine, cols] = grad.astype(BF16)
    for move in kept:
        move.wait()


def back_body(added, place, grad, weight, *refs):
    part = rows_by_rows(grad[...], weight[...])
    if added:
        part = part + refs[0][...].astype(F32)
    outs = refs[added:]
    rows = part.shape[0] // len(outs)
    for h, out in enumerate(outs):
        out[...] = part[h * rows : (h + 1) * rows].astype(out.dtype)


def weight_grad_body(place, left, right, out, mark):
    mark[...] = jnp.zeros_like(mark)
    out[...] = cols_by_cols(left[...], right[...]).astype(BF16)


def gather_exp(block, size):
    distance = size // 2
    by_place = {0: block}
    while distance:
        for place in list(by_place):
            by_place[place ^ distance] = swap(by_place[place], "exp", distance)
        distance //= 2
    return [by_place[k] for k in range(size)]


def per_device(
    queries,
    key_rows,
    value_rows,
    out_grad,
    expert_ids,
    gate_values,
    alibi_slope,
    expert_in,
    expert_out,
):
    BL, features = queries.shape
    G = features // HD
    n = lax.axis_size("seq")
    E = lax.axis_size("exp")
    R = n // G
    cap = 5 * BL // (2 * n)
    stride = -(-cap // 16) * 16
    rows = n * stride
    FFL = expert_in.shape[2]
    L = n * BL
    parts = 2
    each = R // parts
    tall = rows // parts
    half = E // 2
    sizes = (G, R, BL, cap, stride)
    limit = attention_limit(BL, L)
    weight_in = expert_in[0]
    weight_out = expert_out[0]

    ids, gates = expert_ids.T, gate_values.T
    arrays_of = lambda arrays: [
        arrays[h * each] if each == 1 else jnp.concatenate(arrays[h * each : (h + 1) * each], axis=0) for h in range(parts)
    ]

    made = local_call(
        functools.partial(pack_body, sizes),
        [((3 * BL + 16, HD), BF16)] * G + [((G * stride, features), BF16)] * R + [((1,), jnp.int32, pltpu.SMEM)],
        [ids, gates],
        far=[queries, key_rows, value_rows, out_grad],
        scratch=[pltpu.VMEM((4, BL, features), BF16), pltpu.SemaphoreType.DMA((4,))],
        limit=57 * MIB,
        nbytes=6 * BL * features * 2,
    )
    place = made[G + R]
    grad_sent = [swap(made[G + dr], "seq", dr) for dr in range(R)]
    own = [swap(made[d], "seq", d * R) for d in range(G)]
    pairs = [
        own[members[0]][: 2 * BL] if len(members) == 1 else jnp.concatenate([own[d][: 2 * BL] for d in members], axis=0)
        for members in pair_groups(G)
    ]
    others = [swap(piece, "seq", dr) for dr in range(1, R) for piece in pairs]
    block = ((16, HD), (3 * BL // 16, 0))
    routing = local_call(
        functools.partial(routing_body, sizes),
        [((G, rows, BL), BF16)],
        [(own[d], *block) for d in range(G)],
        flops=2 * G * 8 * 4 * BL * BL,
        nbytes=rows * BL * G * 2,
    )[0]

    grad_pieces = local_call(
        functools.partial(column_body, (G, R, stride)),
        [((R * stride, features), BF16)] * G,
        grad_sent,
        after=own[1:],
        nbytes=rows * features * 4,
    )
    kept = [((BL, (i + 1) * R * BL), BF16, pltpu.HBM) for i in range(G)]
    kept += [(shape, BF16, pltpu.HBM) for shape in ((G * BL, HD), (L, HD), (L, HD), (G * BL, HD))]
    shapes = kept + [((G * BL, HD), BF16)]
    made = local_call(
        functools.partial(forward_body, sizes),
        shapes,
        own + others,
        scalars=[alibi_slope],
        scratch=[pltpu.VMEM(x[0], x[1]) for x in kept] + [pltpu.SemaphoreType.DMA((G + 4,))],
        flops=0,
        nbytes=0,
        limit=limit,
    )
    probs = list(made[:G])
    attn, keys, values, query_rows = made[G : G + 4]
    grads = local_call(
        functools.partial(turn_grads_body, (G, R, stride)),
        [((rows, features), BF16)],
        [swap(grad_pieces[dg], "seq", dg * R) for dg in range(G)],
        after=[routing, made[G + 4]],
        nbytes=rows * features * 4,
    )[0]
    grads_far = swap(grads, "exp", half)
    token_sent = local_call(
        functools.partial(dispatch_body, sizes),
        [((R * G * stride, HD), BF16)] * G,
        [made[G + 4], routing],
        flops=2 * rows * BL * HD * G,
        nbytes=2 * MIB,
    )
    token_pieces = [swap(token_sent[dg], "seq", dg * R) for dg in range(G)]
    grad_shards = gather_exp(grads, half) + gather_exp(hold([grads_far], token_pieces[1:] or token_pieces)[0], half)
    width = min(256, FFL)
    steps = FFL // width
    whole = lambda array: (array, array.shape, lambda j, p: (0, 0))
    column_of = lambda array: (array, (array.shape[0], width), lambda j, p: (0, j))
    work = 2 * rows * FFL * features
    through, full_grads = local_call(
        functools.partial(through_body, 1),
        [((rows, FFL), F32), ((rows, E * features), BF16, pltpu.HBM)],
        grad_shards,
        far=[weight_out],
        scratch=[
            pltpu.VMEM((FFL, E * features), BF16),
            pltpu.SemaphoreType.DMA((steps,)),
            pltpu.SemaphoreType.DMA((E,)),
        ],
        flops=work * E,
        nbytes=10 * MIB,
    )

    tokens = local_call(
        functools.partial(turn_tokens_body, (G, R, G * stride)),
        [((G * stride, features), BF16)] * R,
        token_pieces,
        after=[grads_far],
        nbytes=rows * features * 4,
    )
    upper = local_call(
        functools.partial(upper_body, (G, R, BL)),
        [((BL, HD), BF16)] * G,
        [],
        after=tokens[:1],
        far=[out_grad],
        scratch=[pltpu.SemaphoreType.DMA((G,))],
        nbytes=2 * BL * features * 2,
    )
    upper = [swap(upper[d], "seq", d * R) for d in range(G)]

    token_parts = arrays_of([swap(tokens[dr], "seq", dr) for dr in range(R)])
    if G > 1:
        token_parts[1:] = hold(token_parts[1:], upper[1:] + [through])
    far_parts = [swap(part, "exp", half) for part in token_parts]
    near_shards = [gather_exp(part, half) for part in token_parts]
    near_shards = [near_shards[h][k] for k in range(half) for h in range(parts)]
    streamed = [
        pltpu.VMEM((steps, half * features, width), BF16),
        pltpu.SemaphoreType.DMA((half, steps)),
        pltpu.SemaphoreType.DMA((half * parts,)),
    ]
    begun, full_tokens = local_call(
        functools.partial(pre_body, parts, 0),
        [((rows, FFL), F32), ((rows, E * features), BF16, pltpu.HBM)],
        near_shards,
        far=[weight_in],
        scratch=streamed,
        flops=work * half,
        nbytes=8 * MIB,
    )
    far_parts[1:] = hold(far_parts[1:], [begun])
    far_shards = [gather_exp(part, half) for part in far_parts]
    far_shards = [far_shards[h][k] for k in range(half) for h in range(parts)]
    full_tokens, hidden, hidden_grad = local_call(
        functools.partial(pre_body, parts, half),
        [((rows, E * features), BF16, pltpu.HBM)] + [((rows, FFL), BF16)] * 2,
        far_shards + [begun, through],
        into=[full_tokens],
        far=[weight_in],
        aliases={half * parts + 3: 0},
        scratch=streamed,
        flops=work * half,
        nbytes=8 * MIB,
    )

    def back_part(k, moved, count, dtype):
        piece = min(256, features)
        per = features // piece
        added = [] if moved is None else [(moved, (rows, piece), lambda j, p: (0, j))]
        return grid_call(
            functools.partial(back_body, len(added)),
            per,
            place,
            [whole(hidden_grad), (weight_in, (piece, FFL), lambda j, p: ((p[0] ^ k) * per + j, 0))] + added,
            [((rows // count, features), dtype, (rows // count, piece), lambda j, p: (0, j))] * count,
            flops=work,
            nbytes=3 * MIB,
        )

    def summed(first, dtype):
        moved = [swap(back_part(k + 1, None, 1, BF16)[0], "exp", 1) for k in range(first, first + half, 2)]
        return [back_part(first + 2 * at, piece, parts, dtype) for at, piece in enumerate(moved)]

    far = summed(half, BF16)
    arrived = [[swap(piece[h], "exp", half) for h in range(parts)] for piece in far]
    near = summed(0, F32)
    distance = half // 2
    while len(near) > 1:
        count = len(near) // 2
        total = [[near[k][h] + arrived[k][h].astype(F32) for h in range(parts)] for k in range(2 * count)]
        arrived = [[swap(total[count + k][h].astype(BF16), "exp", distance) for h in range(parts)] for k in range(count)]
        near = total[:count]
        distance //= 2

    mark_out = ((8, 128), F32, (8, 128), lambda j, p: (0, 0))
    out_weight_grad, out_mark = grid_call(
        weight_grad_body,
        steps,
        place,
        [column_of(hidden), whole(full_grads)],
        [((FFL, features * E), BF16, (width, features * E), lambda j, p: (j, 0)), mark_out],
        flops=work * E,
        nbytes=10 * MIB,
    )
    count = G * stride
    away = []
    for dr in range(1, R):
        mine = slice((dr % each) * count, (dr % each + 1) * count)
        total = near[0][dr // each][mine] + arrived[0][dr // each][mine].astype(F32)
        away.append(swap(total.astype(BF16), "seq", dr))
    back_sent = local_call(
        functools.partial(turn_back_body, (G, R, count)),
        [((R * count, HD), BF16)] * G,
        [near[0][0], arrived[0][0]] + away,
        after=[out_mark],
        nbytes=tall * features * 8,
    )
    returned = [swap(back_sent[dg], "seq", dg * R) for dg in range(G)]
    in_weight_grad, in_mark = grid_call(
        weight_grad_body,
        E,
        place,
        [(full_tokens, (rows, features), lambda j, p: (0, j)), whole(hidden_grad)],
        [((features * E, FFL), BF16, (features, FFL), lambda j, p: (j, 0)), mark_out],
        flops=work * E,
        nbytes=10 * MIB,
    )

    made = local_call(
        functools.partial(value_body, sizes),
        [((G * BL, HD), BF16)] * (1 + R),
        returned + upper + probs + [routing],
        after=[in_mark],
        scratch=[pltpu.VMEM((L, HD), F32), pltpu.VMEM((G * BL, HD), BF16)],
        flops=2 * G * BL * L * HD,
        nbytes=6 * MIB,
        limit=limit,
    )
    attn_grad, value_parts = made[0], made[1:]
    made = local_call(
        functools.partial(score_body, sizes),
        [((BL, HD), BF16)] * G + [((G * BL, HD), BF16)] * R,
        probs + [attn_grad, attn, keys, values, query_rows],
        scratch=[pltpu.VMEM((G * BL, HD), BF16), pltpu.VMEM((L, HD), F32)],
        flops=6 * G * BL * L * HD,
        nbytes=6 * MIB,
        limit=limit,
    )
    query_pieces, key_parts = made[:G], made[G:]

    def home(pair_parts):
        moved = [swap(pair_parts[dr], "seq", dr) for dr in range(1, R)]
        pieces = []
        for d in range(G):
            mine = slice(d * BL, (d + 1) * BL)
            total = pair_parts[0][mine].astype(F32)
            for piece in moved:
                total = total + piece[mine].astype(F32)
            pieces.append(swap(total.astype(BF16), "seq", d * R))
        return pieces

    value_home = home(value_parts)
    query_home = [swap(query_pieces[d], "seq", d * R) for d in range(G)]
    key_home = home(key_parts)
    query_grad, key_grad, value_grad = local_call(
        functools.partial(unpack_body, (G, R, BL)),
        [((BL, features), BF16)] * 3,
        query_home + key_home + value_home,
        nbytes=6 * BL * features * 2,
    )
    return query_grad, key_grad, value_grad, in_weight_grad[None], out_weight_grad[None]


def solution(mesh):
    return jax.shard_map(
        per_device,
        mesh=mesh,
        in_specs=(
            P("seq", "exp"),
            P("seq", "exp"),
            P("seq", "exp"),
            P("seq", "exp"),
            P("seq", None),
            P("seq", None),
            P("exp"),
            P("seq", None, "exp"),
            P("seq", "exp", None),
        ),
        out_specs=(
            P("seq", "exp"),
            P("seq", "exp"),
            P("seq", "exp"),
            P("seq", None, "exp"),
            P("seq", "exp", None),
        ),
        check_vma=False,
    )
```

```python
import functools
import math

import jax
import jax.numpy as jnp
from jax import lax
from jax.experimental import pallas as pl
from jax.experimental.pallas import tpu as pltpu
from jax.sharding import PartitionSpec as P

HD = 128
WCH = 16
LOG2E = math.log2(math.e)
BF16 = jnp.bfloat16
F32 = jnp.float32
MIB = 1024 * 1024
VMEM_LIMIT = 14 * MIB


def on(pair, dims):
    return lax.dot_general(pair[0], pair[1], ((dims[0], dims[1]), ((), ())), preferred_element_type=F32)


def rows_by_rows(a, b):
    return on((a, b), ((1,), (1,)))


def cols_by_cols(a, b):
    return on((a, b), ((0,), (0,)))


def plain(a, b):
    return on((a, b), ((1,), (0,)))


def swap(block, axis, distance):
    if distance == 0:
        return block
    devices = range(lax.axis_size(axis))
    return lax.ppermute(block, axis, [(i, i ^ distance) for i in devices])


def local_call(body, out_shapes, arrays, scalars=(), after=(), far=(), into=(), aliases=None, scratch=(), flops=0, nbytes=0, limit=VMEM_LIMIT):
    smem = pl.BlockSpec(memory_space=pltpu.SMEM)
    vmem = pl.BlockSpec(memory_space=pltpu.VMEM)
    anywhere = pl.BlockSpec(memory_space=pl.ANY)
    hbm = pl.BlockSpec(memory_space=pltpu.HBM)
    lead = len(scalars)
    grid = (1,) if any(isinstance(x, tuple) for x in arrays) else ()
    specs = [pl.BlockSpec(x[1], lambda j, at=x[2]: at) if isinstance(x, tuple) else vmem for x in arrays] + [hbm] * len(into)
    arrays = [x[0] if isinstance(x, tuple) else x for x in arrays]

    def kernel(*refs):
        body(*refs[:lead], *refs[lead + len(after) :])

    return pl.pallas_call(
        kernel,
        out_shape=[jax.ShapeDtypeStruct(x[0], x[1]) for x in out_shapes],
        grid=grid,
        in_specs=[smem] * lead + [anywhere] * len(after) + [hbm] * len(far) + specs,
        out_specs=[pl.BlockSpec(memory_space=x[2]) if len(x) > 2 else vmem for x in out_shapes],
        scratch_shapes=list(scratch),
        input_output_aliases=aliases or {},
        compiler_params=pltpu.CompilerParams(vmem_limit_bytes=limit),
        cost_estimate=pl.CostEstimate(flops=flops, bytes_accessed=nbytes, transcendentals=0),
    )(*scalars, *after, *far, *arrays, *into)


def hold(arrays, after):
    def body(*refs):
        pass

    anywhere = pl.BlockSpec(memory_space=pl.ANY)
    lead = len(after)
    return list(
        pl.pallas_call(
            body,
            out_shape=[jax.ShapeDtypeStruct(x.shape, x.dtype) for x in arrays],
            in_specs=[anywhere] * (lead + len(arrays)),
            out_specs=[anywhere] * len(arrays),
            input_output_aliases={lead + at: at for at in range(len(arrays))},
            compiler_params=pltpu.CompilerParams(vmem_limit_bytes=MIB),
        )(*after, *arrays)
    )


def grid_call(body, steps, exp_index, ins, outs, after=(), flops=0, nbytes=0, limit=VMEM_LIMIT):
    anywhere = pl.BlockSpec(memory_space=pl.ANY)

    def kernel(place, *refs):
        body(place[0], *refs[len(after) :])

    return pl.pallas_call(
        kernel,
        out_shape=[jax.ShapeDtypeStruct(shape, dtype) for shape, dtype, _, _ in outs],
        grid_spec=pltpu.PrefetchScalarGridSpec(
            num_scalar_prefetch=1,
            grid=(steps,),
            in_specs=[anywhere] * len(after) + [pl.BlockSpec(block, index) for _, block, index in ins],
            out_specs=[pl.BlockSpec(block, index) for _, _, block, index in outs],
        ),
        compiler_params=pltpu.CompilerParams(vmem_limit_bytes=limit),
        cost_estimate=pl.CostEstimate(flops=flops, bytes_accessed=nbytes, transcendentals=0),
    )(exp_index, *after, *[array for array, _, _ in ins])


def attention_limit(block_len, total):
    return min(60 * MIB, 4 * MIB + 6 * block_len * total * 4)


def id_rows_of(ids):
    return [ids[j : j + 1, at : at + 128].astype(F32) for j in range(2) for at in range(0, ids.shape[1], 128)]


def relative_slots(id_rows, place, experts, capacity, stride):
    flat = jnp.concatenate(id_rows, axis=1).astype(jnp.int32)
    entries = flat.shape[1]
    lanes = max(experts, 8)
    one_hot = lax.broadcasted_iota(jnp.int32, (lanes, entries), 0) == flat
    one_hot = one_hot.astype(F32)
    earlier = lax.broadcasted_iota(jnp.int32, (entries, entries), 0) < lax.broadcasted_iota(
        jnp.int32, (entries, entries), 1
    )
    before = plain(one_hot.astype(BF16), earlier.astype(F32).astype(BF16))
    position = jnp.sum(before * one_hot, axis=0, keepdims=True).astype(jnp.int32)
    return jnp.where(position < capacity, (flat ^ place) * stride + position, -1)


def pack_body(sizes, q, k, v, og, ids, gates, *refs):
    G, R, BL = sizes[:3]
    outs, sent, place, held, sems = refs[:G], refs[G : G + R], *refs[G + R :]
    g = lax.axis_index("seq") // R
    place[0] = lax.axis_index("exp")

    moves = [pltpu.make_async_copy(source, held.at[at], sems.at[at]) for at, source in enumerate((k, v, q, og))]
    for move in moves:
        move.start()
    rows = id_rows_of(ids)
    rows.append(jnp.zeros((16 - len(rows), 128), F32))
    rows = jnp.concatenate(rows, axis=0).astype(BF16)
    for d in range(G):
        outs[d][3 * BL : 3 * BL + 16] = rows
    for at, move in enumerate(moves[:3]):
        move.wait()
        for d in range(G):
            cols = pl.ds(pl.multiple_of((g ^ d) * HD, HD), HD)
            outs[d][at * BL : (at + 1) * BL] = held[at, :, cols]
    moves[3].wait()
    route_grads(sizes, held[3], gates, ids, sent)


def upper_body(sizes, og, *refs):
    G, R, BL = sizes
    outs, sems = refs[:G], refs[G]
    g = lax.axis_index("seq") // R
    moves = []
    for d in range(G):
        cols = pl.ds(pl.multiple_of((g ^ d) * HD, HD), HD)
        moves.append(pltpu.make_async_copy(og.at[:, cols], outs[d], sems.at[d]))
    for move in moves:
        move.start()
    for move in moves:
        move.wait()


def route_grads(sizes, block, gates, ids, outs):
    G, R, BL, cap, stride = sizes
    n = G * R
    slots = relative_slots(id_rows_of(ids), lax.axis_index("seq"), n, cap, stride)
    routing = lax.broadcasted_iota(jnp.int32, (n * stride, 2 * BL), 0) == slots
    diagonal = lax.broadcasted_iota(jnp.int32, (BL, BL), 0) == lax.broadcasted_iota(jnp.int32, (BL, BL), 1)
    block = block.astype(F32)
    scaled = []
    for j in range(2):
        gate = jnp.sum(jnp.where(diagonal, gates[j : j + 1], 0.0), axis=1, keepdims=True)
        scaled.append((gate * block).astype(BF16))
    routed = plain(routing.astype(F32).astype(BF16), jnp.concatenate(scaled, axis=0)).astype(BF16)
    for dg in range(G):
        for dr in range(R):
            d = dg * R + dr
            outs[dr][dg * stride : (dg + 1) * stride] = routed[d * stride : (d + 1) * stride]


def routing_body(sizes, *refs):
    G, R, BL, cap, stride = sizes
    n = G * R
    s = lax.axis_index("seq")
    own, out = refs[:G], refs[G]
    for d in range(G):
        rows = own[d][...].astype(F32)
        slots = relative_slots([rows[k : k + 1] for k in range(2 * BL // 128)], s, n, cap, stride)
        slot_rows = lax.broadcasted_iota(jnp.int32, (n * stride, BL), 0)
        chosen = (slot_rows == slots[:, :BL]) | (slot_rows == slots[:, BL:])
        out[pl.ds((s // R) ^ d, 1)] = chosen.astype(F32).astype(BF16)[None]


def pair_groups(G):
    return [members for members in ([0], list(range(1, G))) if members and members[-1] < G]


def forward_body(sizes, slopes, *refs):
    G, R, BL, cap, stride = sizes
    n = G * R
    total = n * BL
    s = lax.axis_index("seq")
    g, r = s // R, s % R
    own, refs = refs[:G], refs[G:]
    groups = pair_groups(G)
    others, refs = refs[: len(groups) * (R - 1)], refs[len(groups) * (R - 1) :]
    far, refs = refs[: G + 4], refs[G + 4 :]
    attn_out, refs = refs[0], refs[1:]
    near, sems = refs[: G + 4], refs[G + 4]
    probs = near[:G]
    attn, keys, values, queries = near[G:]

    def kept(at):
        return pltpu.make_async_copy(near[at], far[at], sems.at[at])

    for d in range(G):
        i = g ^ d
        queries[pl.ds(pl.multiple_of(i * BL, BL), BL)] = own[d][2 * BL : 3 * BL]
        for dr in range(R):
            piece, at = own[d], 0
            if dr:
                group = next(k for k, members in enumerate(groups) if d in members)
                piece = others[(dr - 1) * len(groups) + group]
                at = groups[group].index(d) * 2 * BL
            rows = pl.ds(pl.multiple_of((i * R + (r ^ dr)) * BL, BL), BL)
            keys[rows] = piece[at : at + BL]
            values[rows] = piece[at + BL : at + 2 * BL]
    for at in range(G + 1, G + 4):
        kept(at).start()
    slope = slopes[g]
    span = R * BL
    for i in range(G):
        N = (i + 1) * span
        scores = rows_by_rows(queries[i * BL : (i + 1) * BL], keys[0:N])
        col = lax.broadcasted_iota(jnp.int32, (1, N), 1)
        bias = (col - N).astype(F32) * (slope * LOG2E)
        scores = scores * (HD**-0.5 * LOG2E) + bias
        if total > WCH * BL:
            distance = (
                lax.broadcasted_iota(jnp.int32, (BL, N), 0) + (i * R + r) * BL - lax.broadcasted_iota(jnp.int32, (BL, N), 1)
            )
            scores = jnp.where((distance >= 0) & (distance < WCH * BL), scores, -jnp.inf)
        else:
            ahead = lax.broadcasted_iota(jnp.int32, (BL, span), 1) - lax.broadcasted_iota(jnp.int32, (BL, span), 0)
            last = jnp.where(ahead <= r * BL, scores[:, N - span :], -jnp.inf)
            scores = last if i == 0 else jnp.concatenate([scores[:, : N - span], last], axis=1)
        top = jnp.max(scores, axis=1, keepdims=True)
        grown = jnp.exp2(scores - top)
        norm = jnp.sum(grown, axis=1, keepdims=True)
        weights = (grown * (1.0 / norm)).astype(BF16)
        probs[i][...] = weights
        kept(i).start()
        out = plain(weights, values[0:N]).astype(BF16)
        attn[i * BL : (i + 1) * BL] = out
        attn_out[i * BL : (i + 1) * BL] = out
    kept(G).start()
    for at in range(G + 4):
        kept(at).wait()


def dispatch_body(sizes, attn, routing, *sent):
    G, R, BL, cap, stride = sizes
    for i in range(G):
        routed = plain(routing[i], attn[i * BL : (i + 1) * BL]).astype(BF16)
        for dg in range(G):
            for dr in range(R):
                d = dg * R + dr
                at = (dr * G + i) * stride
                sent[dg][at : at + stride] = routed[d * stride : (d + 1) * stride]


def value_body(sizes, *refs):
    G, R, BL, cap, stride = sizes
    n = G * R
    s = lax.axis_index("seq")
    g, r = s // R, s % R
    back, refs = refs[:n], refs[n:]
    upper, refs = refs[:G], refs[G:]
    probs, refs = refs[:G], refs[G:]
    routing, attn_grad, refs = refs[0], refs[1], refs[2:]
    outs, total, upper_rows = refs[:R], refs[R], refs[R + 1]
    for d in range(G):
        upper_rows[pl.ds(pl.multiple_of((g ^ d) * BL, BL), BL)] = upper[d][...]
    for i in reversed(range(G)):
        N = (i + 1) * R * BL
        mine = slice(i * BL, (i + 1) * BL)
        rows = jnp.concatenate([back[d][i * stride : (i + 1) * stride] for d in range(n)], axis=0)
        picked = cols_by_cols(routing[i], rows)
        grad = (upper_rows[mine].astype(F32) + picked).astype(BF16)
        attn_grad[mine] = grad
        part = cols_by_cols(probs[i][...], grad)
        if i == G - 1:
            total[...] = part
        else:
            total[0:N] += part
    spread(sizes, total, outs)


def spread(sizes, total, outs):
    G, R, BL = sizes[:3]
    s = lax.axis_index("seq")
    g, r = s // R, s % R
    for d in range(G):
        for dr in range(R):
            rows = pl.ds(pl.multiple_of(((g ^ d) * R + (r ^ dr)) * BL, BL), BL)
            outs[dr][d * BL : (d + 1) * BL] = total[rows].astype(BF16)


def score_body(sizes, *refs):
    G, R, BL = sizes[:3]
    s = lax.axis_index("seq")
    g = s // R
    probs, refs = refs[:G], refs[G:]
    attn_grad, attn, keys, values, queries = refs[:5]
    refs = refs[5:]
    query_out, refs = refs[:G], refs[G:]
    outs, query_rows, total = refs[:R], refs[R], refs[R + 1]
    scale = HD**-0.5
    for i in reversed(range(G)):
        N = (i + 1) * R * BL
        mine = slice(i * BL, (i + 1) * BL)
        grad = attn_grad[mine]
        delta = jnp.sum(grad.astype(F32) * attn[mine].astype(F32), axis=1, keepdims=True)
        dprob = rows_by_rows(grad, values[0:N])
        dscore = (probs[i][...].astype(F32) * (dprob - delta)).astype(BF16)
        query_rows[mine] = (plain(dscore, keys[0:N]) * scale).astype(BF16)
        part = cols_by_cols(dscore, queries[mine]) * scale
        if i == G - 1:
            total[...] = part
        else:
            total[0:N] += part
    for d in range(G):
        query_out[d][...] = query_rows[pl.ds(pl.multiple_of((g ^ d) * BL, BL), BL)]
    spread(sizes, total, outs)


def unpack_body(sizes, *refs):
    G, R, BL = sizes
    g = lax.axis_index("seq") // R
    pieces, outs = refs[: 3 * G], refs[3 * G :]
    for at in range(3):
        for d in range(G):
            cols = pl.ds(pl.multiple_of((g ^ d) * HD, HD), HD)
            outs[at][:, cols] = pieces[at * G + d][...]


def turn_tokens_body(sizes, *refs):
    G, R, count = sizes
    g = lax.axis_index("seq") // R
    for dg in range(G):
        cols = pl.ds(pl.multiple_of((g ^ dg) * HD, HD), HD)
        for dr in range(R):
            refs[G + dr][:, cols] = refs[dg][dr * count : (dr + 1) * count]


def column_body(sizes, *refs):
    G, R, stride = sizes
    for dg in range(G):
        for dr in range(R):
            refs[R + dg][dr * stride : (dr + 1) * stride] = refs[dr][dg * stride : (dg + 1) * stride]


def turn_grads_body(sizes, *refs):
    G, R, stride = sizes
    g = lax.axis_index("seq") // R
    for dg in range(G):
        for dr in range(R):
            at = pl.ds(pl.multiple_of((dr * G + (g ^ dg)) * stride, 16), stride)
            refs[-1][at] = refs[dg][dr * stride : (dr + 1) * stride]


def turn_back_body(sizes, near, arrived, *outs):
    G, R, count = sizes
    g = lax.axis_index("seq") // R
    each = len(outs) // G
    for dg in range(G):
        cols = pl.ds(pl.multiple_of((g ^ dg) * HD, HD), HD)
        for at in range(each):
            rows = slice(at * count, (at + 1) * count)
            outs[dg * each + at][...] = (near[rows, cols] + arrived[rows, cols].astype(F32)).astype(BF16)


def keep_moves(parts, first, shards, full, sems):
    place = lax.axis_index("exp")
    rows, width = shards[0].shape
    moves = []
    for at, shard in enumerate(shards):
        k, h = first + at // parts, at % parts
        cols = pl.ds(pl.multiple_of((place ^ k) * width, 128), width)
        moves.append(pltpu.make_async_copy(shard, full.at[pl.ds(h * rows, rows), cols], sems.at[at]))
    return moves


def through_body(parts, weight, *refs):
    shards, out, full, held, sems, own_sems = refs[:-5], *refs[-5:]
    place = lax.axis_index("exp")
    rows, width = shards[0].shape
    steps = sems.shape[0]
    kept = keep_moves(parts, 0, shards, full, own_sems)
    tall = weight.shape[0] // steps

    def fetch(c):
        mine = pl.ds(c * tall, tall)
        return pltpu.make_async_copy(weight.at[mine], held.at[mine], sems.at[c])

    for c in range(min(2, steps)):
        fetch(c).start()
    for move in kept:
        move.start()
    for c in range(steps):
        fetch(c).wait()
        if c + 2 < steps:
            fetch(c + 2).start()
        for h in range(parts):
            total = None
            for k in range(len(shards) // parts):
                cols = pl.ds(pl.multiple_of((place ^ k) * width, 128), width)
                part = rows_by_rows(shards[k * parts + h][...], held[c * tall : (c + 1) * tall, cols])
                total = part if total is None else total + part
            out[h * rows : (h + 1) * rows, c * tall : (c + 1) * tall] = total
    for move in kept:
        move.wait()


def pre_body(parts, weight, *refs):
    shards, through, full, hidden, hidden_grad, held, sems, own_sems = refs[:-7], *refs[-7:]
    place = lax.axis_index("exp")
    rows, width = shards[0].shape
    steps = sems.shape[0]
    wide = weight.shape[1] // steps
    kept = keep_moves(parts, 0, shards, full, own_sems)

    def fetch(c):
        return pltpu.make_async_copy(weight.at[:, pl.ds(c * wide, wide)], held.at[c], sems.at[c])

    for c in range(min(2, steps)):
        fetch(c).start()
    for move in kept:
        move.start()
    for c in range(steps):
        cols = slice(c * wide, (c + 1) * wide)
        fetch(c).wait()
        if c + 2 < steps:
            fetch(c + 2).start()
        for h in range(parts):
            mine = slice(h * rows, (h + 1) * rows)
            total = None
            for k in range(len(shards) // parts):
                at = pl.ds(pl.multiple_of((place ^ k) * width, 128), width)
                part = plain(shards[k * parts + h][...], held[c, at, :])
                total = part if total is None else total + part
            logistic = 1.0 / (1.0 + jnp.exp(-total))
            hidden[mine, cols] = (total * logistic).astype(BF16)
            grad = through[mine, cols] * logistic * (1.0 + total * (1.0 - logistic))
            hidden_grad[mine, cols] = grad.astype(BF16)
    for move in kept:
        move.wait()


def back_body(added, place, grad, weight, *refs):
    part = rows_by_rows(grad[...], weight[...])
    if added:
        part = part + refs[0][...].astype(F32)
    outs = refs[added:]
    rows = part.shape[0] // len(outs)
    for h, out in enumerate(outs):
        out[...] = part[h * rows : (h + 1) * rows].astype(out.dtype)


def weight_grad_body(place, left, right, out, mark):
    mark[...] = jnp.zeros_like(mark)
    out[...] = cols_by_cols(left[...], right[...]).astype(BF16)


def gather_exp(block, size):
    distance = size // 2
    by_place = {0: block}
    while distance:
        for place in list(by_place):
            by_place[place ^ distance] = swap(by_place[place], "exp", distance)
        distance //= 2
    return [by_place[k] for k in range(size)]


def per_device(
    queries,
    key_rows,
    value_rows,
    out_grad,
    expert_ids,
    gate_values,
    alibi_slope,
    expert_in,
    expert_out,
):
    BL, features = queries.shape
    G = features // HD
    n = lax.axis_size("seq")
    E = lax.axis_size("exp")
    R = n // G
    cap = 5 * BL // (2 * n)
    stride = -(-cap // 16) * 16
    rows = n * stride
    FFL = expert_in.shape[2]
    L = n * BL
    parts = 2
    each = R // parts
    tall = rows // parts
    half = E // 2
    sizes = (G, R, BL, cap, stride)
    limit = attention_limit(BL, L)
    weight_in = expert_in[0]
    weight_out = expert_out[0]

    ids, gates = expert_ids.T, gate_values.T
    arrays_of = lambda arrays: [
        arrays[h * each] if each == 1 else jnp.concatenate(arrays[h * each : (h + 1) * each], axis=0) for h in range(parts)
    ]

    made = local_call(
        functools.partial(pack_body, sizes),
        [((3 * BL + 16, HD), BF16)] * G + [((G * stride, features), BF16)] * R + [((1,), jnp.int32, pltpu.SMEM)],
        [ids, gates],
        far=[queries, key_rows, value_rows, out_grad],
        scratch=[pltpu.VMEM((4, BL, features), BF16), pltpu.SemaphoreType.DMA((4,))],
        limit=57 * MIB,
        nbytes=6 * BL * features * 2,
    )
    place = made[G + R]
    grad_sent = [swap(made[G + dr], "seq", dr) for dr in range(R)]
    own = [swap(made[d], "seq", d * R) for d in range(G)]
    pairs = [
        own[members[0]][: 2 * BL] if len(members) == 1 else jnp.concatenate([own[d][: 2 * BL] for d in members], axis=0)
        for members in pair_groups(G)
    ]
    others = [swap(piece, "seq", dr) for dr in range(1, R) for piece in pairs]
    block = ((16, HD), (3 * BL // 16, 0))
    routing = local_call(
        functools.partial(routing_body, sizes),
        [((G, rows, BL), BF16)],
        [(own[d], *block) for d in range(G)],
        flops=2 * G * 8 * 4 * BL * BL,
        nbytes=rows * BL * G * 2,
    )[0]

    grad_pieces = local_call(
        functools.partial(column_body, (G, R, stride)),
        [((R * stride, features), BF16)] * G,
        grad_sent,
        after=own[1:],
        nbytes=rows * features * 4,
    )
    kept = [((BL, (i + 1) * R * BL), BF16, pltpu.HBM) for i in range(G)]
    kept += [(shape, BF16, pltpu.HBM) for shape in ((G * BL, HD), (L, HD), (L, HD), (G * BL, HD))]
    shapes = kept + [((G * BL, HD), BF16)]
    made = local_call(
        functools.partial(forward_body, sizes),
        shapes,
        own + others,
        scalars=[alibi_slope],
        scratch=[pltpu.VMEM(x[0], x[1]) for x in kept] + [pltpu.SemaphoreType.DMA((G + 4,))],
        flops=0,
        nbytes=0,
        limit=limit,
    )
    probs = list(made[:G])
    attn, keys, values, query_rows = made[G : G + 4]
    grads = local_call(
        functools.partial(turn_grads_body, (G, R, stride)),
        [((rows, features), BF16)],
        [swap(grad_pieces[dg], "seq", dg * R) for dg in range(G)],
        after=[routing, made[G + 4]],
        nbytes=rows * features * 4,
    )[0]
    grads_far = swap(grads, "exp", half)
    token_sent = local_call(
        functools.partial(dispatch_body, sizes),
        [((R * G * stride, HD), BF16)] * G,
        [made[G + 4], routing],
        flops=2 * rows * BL * HD * G,
        nbytes=2 * MIB,
    )
    token_pieces = [swap(token_sent[dg], "seq", dg * R) for dg in range(G)]
    grad_shards = gather_exp(grads, half) + gather_exp(hold([grads_far], token_pieces[1:] or token_pieces)[0], half)
    width = min(256, FFL)
    steps = FFL // width
    whole = lambda array: (array, array.shape, lambda j, p: (0, 0))
    column_of = lambda array: (array, (array.shape[0], width), lambda j, p: (0, j))
    work = 2 * rows * FFL * features
    through, full_grads = local_call(
        functools.partial(through_body, 1),
        [((rows, FFL), F32), ((rows, E * features), BF16, pltpu.HBM)],
        grad_shards,
        far=[weight_out],
        scratch=[
            pltpu.VMEM((FFL, E * features), BF16),
            pltpu.SemaphoreType.DMA((steps,)),
            pltpu.SemaphoreType.DMA((E,)),
        ],
        flops=work * E,
        nbytes=10 * MIB,
    )

    tokens = local_call(
        functools.partial(turn_tokens_body, (G, R, G * stride)),
        [((G * stride, features), BF16)] * R,
        token_pieces,
        after=[grads_far],
        nbytes=rows * features * 4,
    )
    token_parts = arrays_of([swap(tokens[dr], "seq", dr) for dr in range(R)])
    token_parts[1:] = hold(token_parts[1:], [through])
    upper = local_call(
        functools.partial(upper_body, (G, R, BL)),
        [((BL, HD), BF16)] * G,
        [],
        after=token_parts[1:],
        far=[out_grad],
        scratch=[pltpu.SemaphoreType.DMA((G,))],
        nbytes=2 * BL * features * 2,
    )
    upper = [swap(upper[d], "seq", d * R) for d in range(G)]
    far_parts = [swap(part, "exp", half) for part in token_parts]
    if G > 1:
        far_parts[1:] = hold(far_parts[1:], upper[1:])
    near_shards = [gather_exp(part, half) for part in token_parts]
    near_shards = [near_shards[h][k] for k in range(half) for h in range(parts)]
    far_shards = [gather_exp(part, half) for part in far_parts]
    far_shards = [far_shards[h][k] for k in range(half) for h in range(parts)]
    full_tokens, hidden, hidden_grad = local_call(
        functools.partial(pre_body, parts),
        [((rows, E * features), BF16, pltpu.HBM)] + [((rows, FFL), BF16)] * 2,
        near_shards + far_shards + [through],
        far=[weight_in],
        scratch=[
            pltpu.VMEM((steps, E * features, width), BF16),
            pltpu.SemaphoreType.DMA((steps,)),
            pltpu.SemaphoreType.DMA((E * parts,)),
        ],
        flops=work * E,
        nbytes=8 * MIB,
    )

    def back_part(k, moved, count, dtype):
        piece = min(256, features)
        per = features // piece
        added = [] if moved is None else [(moved, (rows, piece), lambda j, p: (0, j))]
        return grid_call(
            functools.partial(back_body, len(added)),
            per,
            place,
            [whole(hidden_grad), (weight_in, (piece, FFL), lambda j, p: ((p[0] ^ k) * per + j, 0))] + added,
            [((rows // count, features), dtype, (rows // count, piece), lambda j, p: (0, j))] * count,
            flops=work,
            nbytes=3 * MIB,
        )

    def summed(first, dtype):
        moved = [swap(back_part(k + 1, None, 1, BF16)[0], "exp", 1) for k in range(first, first + half, 2)]
        return [back_part(first + 2 * at, piece, parts, dtype) for at, piece in enumerate(moved)]

    far = summed(half, BF16)
    arrived = [[swap(piece[h], "exp", half) for h in range(parts)] for piece in far]
    near = summed(0, F32)
    distance = half // 2
    while len(near) > 1:
        count = len(near) // 2
        total = [[near[k][h] + arrived[k][h].astype(F32) for h in range(parts)] for k in range(2 * count)]
        arrived = [[swap(total[count + k][h].astype(BF16), "exp", distance) for h in range(parts)] for k in range(count)]
        near = total[:count]
        distance //= 2

    mark_out = ((8, 128), F32, (8, 128), lambda j, p: (0, 0))
    out_weight_grad, out_mark = grid_call(
        weight_grad_body,
        steps,
        place,
        [column_of(hidden), whole(full_grads)],
        [((FFL, features * E), BF16, (width, features * E), lambda j, p: (j, 0)), mark_out],
        flops=work * E,
        nbytes=10 * MIB,
    )
    returned = [None] * n
    ready = [out_mark]
    for h in range(parts):
        pieces = local_call(
            functools.partial(turn_back_body, (G, R, G * stride)),
            [((G * stride, HD), BF16)] * (G * each),
            [near[0][h], arrived[0][h]],
            after=ready,
            nbytes=tall * features * 8,
        )
        for dg in range(G):
            for at in range(each):
                d = dg * R + h * each + at
                returned[d] = swap(pieces[dg * each + at], "seq", d)
        ready = [x for x in returned[1:] if x is not None]
    in_weight_grad, in_mark = grid_call(
        weight_grad_body,
        E,
        place,
        [(full_tokens, (rows, features), lambda j, p: (0, j)), whole(hidden_grad)],
        [((features * E, FFL), BF16, (features, FFL), lambda j, p: (j, 0)), mark_out],
        flops=work * E,
        nbytes=10 * MIB,
    )

    made = local_call(
        functools.partial(value_body, sizes),
        [((G * BL, HD), BF16)] * (1 + R),
        returned + upper + probs + [routing],
        after=[in_mark],
        scratch=[pltpu.VMEM((L, HD), F32), pltpu.VMEM((G * BL, HD), BF16)],
        flops=2 * G * BL * L * HD,
        nbytes=6 * MIB,
        limit=limit,
    )
    attn_grad, value_parts = made[0], made[1:]
    made = local_call(
        functools.partial(score_body, sizes),
        [((BL, HD), BF16)] * G + [((G * BL, HD), BF16)] * R,
        probs + [attn_grad, attn, keys, values, query_rows],
        scratch=[pltpu.VMEM((G * BL, HD), BF16), pltpu.VMEM((L, HD), F32)],
        flops=6 * G * BL * L * HD,
        nbytes=6 * MIB,
        limit=limit,
    )
    query_pieces, key_parts = made[:G], made[G:]

    def home(pair_parts):
        moved = [swap(pair_parts[dr], "seq", dr) for dr in range(1, R)]
        pieces = []
        for d in range(G):
            mine = slice(d * BL, (d + 1) * BL)
            total = pair_parts[0][mine].astype(F32)
            for piece in moved:
                total = total + piece[mine].astype(F32)
            pieces.append(swap(total.astype(BF16), "seq", d * R))
        return pieces

    value_home = home(value_parts)
    query_home = [swap(query_pieces[d], "seq", d * R) for d in range(G)]
    key_home = home(key_parts)
    query_grad, key_grad, value_grad = local_call(
        functools.partial(unpack_body, (G, R, BL)),
        [((BL, features), BF16)] * 3,
        query_home + key_home + value_home,
        nbytes=6 * BL * features * 2,
    )
    return query_grad, key_grad, value_grad, in_weight_grad[None], out_weight_grad[None]


def solution(mesh):
    return jax.shard_map(
        per_device,
        mesh=mesh,
        in_specs=(
            P("seq", "exp"),
            P("seq", "exp"),
            P("seq", "exp"),
            P("seq", "exp"),
            P("seq", None),
            P("seq", None),
            P("exp"),
            P("seq", None, "exp"),
            P("seq", "exp", None),
        ),
        out_specs=(
            P("seq", "exp"),
            P("seq", "exp"),
            P("seq", "exp"),
            P("seq", None, "exp"),
            P("seq", "exp", None),
        ),
        check_vma=False,
    )
```

```python
import functools
import math

import jax
import jax.numpy as jnp
from jax import lax
from jax.experimental import pallas as pl
from jax.experimental.pallas import tpu as pltpu
from jax.sharding import PartitionSpec as P

HD = 128
WCH = 16
LOG2E = math.log2(math.e)
BF16 = jnp.bfloat16
F32 = jnp.float32
MIB = 1024 * 1024
VMEM_LIMIT = 14 * MIB


def on(pair, dims):
    return lax.dot_general(pair[0], pair[1], ((dims[0], dims[1]), ((), ())), preferred_element_type=F32)


def rows_by_rows(a, b):
    return on((a, b), ((1,), (1,)))


def cols_by_cols(a, b):
    return on((a, b), ((0,), (0,)))


def plain(a, b):
    return on((a, b), ((1,), (0,)))


def swap(block, axis, distance):
    if distance == 0:
        return block
    devices = range(lax.axis_size(axis))
    return lax.ppermute(block, axis, [(i, i ^ distance) for i in devices])


def local_call(body, out_shapes, arrays, scalars=(), after=(), far=(), into=(), aliases=None, scratch=(), flops=0, nbytes=0, limit=VMEM_LIMIT):
    smem = pl.BlockSpec(memory_space=pltpu.SMEM)
    vmem = pl.BlockSpec(memory_space=pltpu.VMEM)
    anywhere = pl.BlockSpec(memory_space=pl.ANY)
    hbm = pl.BlockSpec(memory_space=pltpu.HBM)
    lead = len(scalars)
    grid = (1,) if any(isinstance(x, tuple) for x in arrays) else ()
    specs = [pl.BlockSpec(x[1], lambda j, at=x[2]: at) if isinstance(x, tuple) else vmem for x in arrays] + [hbm] * len(into)
    arrays = [x[0] if isinstance(x, tuple) else x for x in arrays]

    def kernel(*refs):
        body(*refs[:lead], *refs[lead + len(after) :])

    return pl.pallas_call(
        kernel,
        out_shape=[jax.ShapeDtypeStruct(x[0], x[1]) for x in out_shapes],
        grid=grid,
        in_specs=[smem] * lead + [anywhere] * len(after) + [hbm] * len(far) + specs,
        out_specs=[pl.BlockSpec(memory_space=x[2]) if len(x) > 2 else vmem for x in out_shapes],
        scratch_shapes=list(scratch),
        input_output_aliases=aliases or {},
        compiler_params=pltpu.CompilerParams(vmem_limit_bytes=limit),
        cost_estimate=pl.CostEstimate(flops=flops, bytes_accessed=nbytes, transcendentals=0),
    )(*scalars, *after, *far, *arrays, *into)


def hold(arrays, after):
    def body(*refs):
        pass

    anywhere = pl.BlockSpec(memory_space=pl.ANY)
    lead = len(after)
    return list(
        pl.pallas_call(
            body,
            out_shape=[jax.ShapeDtypeStruct(x.shape, x.dtype) for x in arrays],
            in_specs=[anywhere] * (lead + len(arrays)),
            out_specs=[anywhere] * len(arrays),
            input_output_aliases={lead + at: at for at in range(len(arrays))},
            compiler_params=pltpu.CompilerParams(vmem_limit_bytes=MIB),
        )(*after, *arrays)
    )


def grid_call(body, steps, exp_index, ins, outs, after=(), flops=0, nbytes=0, limit=VMEM_LIMIT):
    anywhere = pl.BlockSpec(memory_space=pl.ANY)

    def kernel(place, *refs):
        body(place[0], *refs[len(after) :])

    return pl.pallas_call(
        kernel,
        out_shape=[jax.ShapeDtypeStruct(shape, dtype) for shape, dtype, _, _ in outs],
        grid_spec=pltpu.PrefetchScalarGridSpec(
            num_scalar_prefetch=1,
            grid=(steps,),
            in_specs=[anywhere] * len(after) + [pl.BlockSpec(block, index) for _, block, index in ins],
            out_specs=[pl.BlockSpec(block, index) for _, _, block, index in outs],
        ),
        compiler_params=pltpu.CompilerParams(vmem_limit_bytes=limit),
        cost_estimate=pl.CostEstimate(flops=flops, bytes_accessed=nbytes, transcendentals=0),
    )(exp_index, *after, *[array for array, _, _ in ins])


def attention_limit(block_len, total):
    return min(60 * MIB, 4 * MIB + 6 * block_len * total * 4)


def id_rows_of(ids):
    return [ids[j : j + 1, at : at + 128].astype(F32) for j in range(2) for at in range(0, ids.shape[1], 128)]


def relative_slots(id_rows, place, experts, capacity, stride):
    flat = jnp.concatenate(id_rows, axis=1).astype(jnp.int32)
    entries = flat.shape[1]
    lanes = max(experts, 8)
    one_hot = lax.broadcasted_iota(jnp.int32, (lanes, entries), 0) == flat
    one_hot = one_hot.astype(F32)
    earlier = lax.broadcasted_iota(jnp.int32, (entries, entries), 0) < lax.broadcasted_iota(
        jnp.int32, (entries, entries), 1
    )
    before = plain(one_hot.astype(BF16), earlier.astype(F32).astype(BF16))
    position = jnp.sum(before * one_hot, axis=0, keepdims=True).astype(jnp.int32)
    return jnp.where(position < capacity, (flat ^ place) * stride + position, -1)


def pack_body(sizes, q, k, v, og, ids, gates, *refs):
    G, R, BL = sizes[:3]
    outs, sent, place, held, sems = refs[:G], refs[G : G + R], *refs[G + R :]
    g = lax.axis_index("seq") // R
    place[0] = lax.axis_index("exp")

    moves = [pltpu.make_async_copy(source, held.at[at], sems.at[at]) for at, source in enumerate((k, v, q, og))]
    for move in moves:
        move.start()
    rows = id_rows_of(ids)
    rows.append(jnp.zeros((16 - len(rows), 128), F32))
    rows = jnp.concatenate(rows, axis=0).astype(BF16)
    for d in range(G):
        outs[d][3 * BL : 3 * BL + 16] = rows
    for at, move in enumerate(moves[:3]):
        move.wait()
        for d in range(G):
            cols = pl.ds(pl.multiple_of((g ^ d) * HD, HD), HD)
            outs[d][at * BL : (at + 1) * BL] = held[at, :, cols]
    moves[3].wait()
    route_grads(sizes, held[3], gates, ids, sent)


def upper_body(sizes, og, *refs):
    G, R, BL = sizes
    outs, sems = refs[:G], refs[G]
    g = lax.axis_index("seq") // R
    moves = []
    for d in range(G):
        cols = pl.ds(pl.multiple_of((g ^ d) * HD, HD), HD)
        moves.append(pltpu.make_async_copy(og.at[:, cols], outs[d], sems.at[d]))
    for move in moves:
        move.start()
    for move in moves:
        move.wait()


def route_grads(sizes, block, gates, ids, outs):
    G, R, BL, cap, stride = sizes
    n = G * R
    slots = relative_slots(id_rows_of(ids), lax.axis_index("seq"), n, cap, stride)
    routing = lax.broadcasted_iota(jnp.int32, (n * stride, 2 * BL), 0) == slots
    diagonal = lax.broadcasted_iota(jnp.int32, (BL, BL), 0) == lax.broadcasted_iota(jnp.int32, (BL, BL), 1)
    block = block.astype(F32)
    scaled = []
    for j in range(2):
        gate = jnp.sum(jnp.where(diagonal, gates[j : j + 1], 0.0), axis=1, keepdims=True)
        scaled.append((gate * block).astype(BF16))
    routed = plain(routing.astype(F32).astype(BF16), jnp.concatenate(scaled, axis=0)).astype(BF16)
    for dg in range(G):
        for dr in range(R):
            d = dg * R + dr
            outs[dr][dg * stride : (dg + 1) * stride] = routed[d * stride : (d + 1) * stride]


def routing_body(sizes, *refs):
    G, R, BL, cap, stride = sizes
    n = G * R
    s = lax.axis_index("seq")
    own, out = refs[:G], refs[G]
    for d in range(G):
        rows = own[d][...].astype(F32)
        slots = relative_slots([rows[k : k + 1] for k in range(2 * BL // 128)], s, n, cap, stride)
        slot_rows = lax.broadcasted_iota(jnp.int32, (n * stride, BL), 0)
        chosen = (slot_rows == slots[:, :BL]) | (slot_rows == slots[:, BL:])
        out[pl.ds((s // R) ^ d, 1)] = chosen.astype(F32).astype(BF16)[None]


def pair_groups(G):
    return [members for members in ([0], list(range(1, G))) if members and members[-1] < G]


def forward_body(sizes, slopes, *refs):
    G, R, BL, cap, stride = sizes
    n = G * R
    total = n * BL
    s = lax.axis_index("seq")
    g, r = s // R, s % R
    own, refs = refs[:G], refs[G:]
    groups = pair_groups(G)
    others, refs = refs[: len(groups) * (R - 1)], refs[len(groups) * (R - 1) :]
    far, refs = refs[: G + 4], refs[G + 4 :]
    attn_out, refs = refs[0], refs[1:]
    near, sems = refs[: G + 4], refs[G + 4]
    probs = near[:G]
    attn, keys, values, queries = near[G:]

    def kept(at):
        return pltpu.make_async_copy(near[at], far[at], sems.at[at])

    for d in range(G):
        i = g ^ d
        queries[pl.ds(pl.multiple_of(i * BL, BL), BL)] = own[d][2 * BL : 3 * BL]
        for dr in range(R):
            piece, at = own[d], 0
            if dr:
                group = next(k for k, members in enumerate(groups) if d in members)
                piece = others[(dr - 1) * len(groups) + group]
                at = groups[group].index(d) * 2 * BL
            rows = pl.ds(pl.multiple_of((i * R + (r ^ dr)) * BL, BL), BL)
            keys[rows] = piece[at : at + BL]
            values[rows] = piece[at + BL : at + 2 * BL]
    for at in range(G + 1, G + 4):
        kept(at).start()
    slope = slopes[g]
    span = R * BL
    for i in range(G):
        N = (i + 1) * span
        scores = rows_by_rows(queries[i * BL : (i + 1) * BL], keys[0:N])
        col = lax.broadcasted_iota(jnp.int32, (1, N), 1)
        bias = (col - N).astype(F32) * (slope * LOG2E)
        scores = scores * (HD**-0.5 * LOG2E) + bias
        if total > WCH * BL:
            distance = (
                lax.broadcasted_iota(jnp.int32, (BL, N), 0) + (i * R + r) * BL - lax.broadcasted_iota(jnp.int32, (BL, N), 1)
            )
            scores = jnp.where((distance >= 0) & (distance < WCH * BL), scores, -jnp.inf)
        else:
            ahead = lax.broadcasted_iota(jnp.int32, (BL, span), 1) - lax.broadcasted_iota(jnp.int32, (BL, span), 0)
            last = jnp.where(ahead <= r * BL, scores[:, N - span :], -jnp.inf)
            scores = last if i == 0 else jnp.concatenate([scores[:, : N - span], last], axis=1)
        top = jnp.max(scores, axis=1, keepdims=True)
        grown = jnp.exp2(scores - top)
        norm = jnp.sum(grown, axis=1, keepdims=True)
        weights = (grown * (1.0 / norm)).astype(BF16)
        probs[i][...] = weights
        kept(i).start()
        out = plain(weights, values[0:N]).astype(BF16)
        attn[i * BL : (i + 1) * BL] = out
        attn_out[i * BL : (i + 1) * BL] = out
    kept(G).start()
    for at in range(G + 4):
        kept(at).wait()


def dispatch_body(sizes, attn, routing, *sent):
    G, R, BL, cap, stride = sizes
    for i in range(G):
        routed = plain(routing[i], attn[i * BL : (i + 1) * BL]).astype(BF16)
        for dg in range(G):
            for dr in range(R):
                d = dg * R + dr
                at = (dr * G + i) * stride
                sent[dg][at : at + stride] = routed[d * stride : (d + 1) * stride]


def value_body(sizes, *refs):
    G, R, BL, cap, stride = sizes
    n = G * R
    s = lax.axis_index("seq")
    g, r = s // R, s % R
    back, refs = refs[:n], refs[n:]
    upper, refs = refs[:G], refs[G:]
    probs, refs = refs[:G], refs[G:]
    routing, attn_grad, refs = refs[0], refs[1], refs[2:]
    outs, total, upper_rows = refs[:R], refs[R], refs[R + 1]
    for d in range(G):
        upper_rows[pl.ds(pl.multiple_of((g ^ d) * BL, BL), BL)] = upper[d][...]
    for i in reversed(range(G)):
        N = (i + 1) * R * BL
        mine = slice(i * BL, (i + 1) * BL)
        rows = jnp.concatenate([back[d][i * stride : (i + 1) * stride] for d in range(n)], axis=0)
        picked = cols_by_cols(routing[i], rows)
        grad = (upper_rows[mine].astype(F32) + picked).astype(BF16)
        attn_grad[mine] = grad
        part = cols_by_cols(probs[i][...], grad)
        if i == G - 1:
            total[...] = part
        else:
            total[0:N] += part
    spread(sizes, total, outs)


def spread(sizes, total, outs):
    G, R, BL = sizes[:3]
    s = lax.axis_index("seq")
    g, r = s // R, s % R
    for d in range(G):
        for dr in range(R):
            rows = pl.ds(pl.multiple_of(((g ^ d) * R + (r ^ dr)) * BL, BL), BL)
            outs[dr][d * BL : (d + 1) * BL] = total[rows].astype(BF16)


def score_body(sizes, *refs):
    G, R, BL = sizes[:3]
    s = lax.axis_index("seq")
    g = s // R
    probs, refs = refs[:G], refs[G:]
    attn_grad, attn, keys, values, queries = refs[:5]
    refs = refs[5:]
    query_out, refs = refs[:G], refs[G:]
    outs, query_rows, total = refs[:R], refs[R], refs[R + 1]
    scale = HD**-0.5
    for i in reversed(range(G)):
        N = (i + 1) * R * BL
        mine = slice(i * BL, (i + 1) * BL)
        grad = attn_grad[mine]
        delta = jnp.sum(grad.astype(F32) * attn[mine].astype(F32), axis=1, keepdims=True)
        dprob = rows_by_rows(grad, values[0:N])
        dscore = (probs[i][...].astype(F32) * (dprob - delta)).astype(BF16)
        query_rows[mine] = (plain(dscore, keys[0:N]) * scale).astype(BF16)
        part = cols_by_cols(dscore, queries[mine]) * scale
        if i == G - 1:
            total[...] = part
        else:
            total[0:N] += part
    for d in range(G):
        query_out[d][...] = query_rows[pl.ds(pl.multiple_of((g ^ d) * BL, BL), BL)]
    spread(sizes, total, outs)


def unpack_body(sizes, *refs):
    G, R, BL = sizes
    g = lax.axis_index("seq") // R
    pieces, outs = refs[: 3 * G], refs[3 * G :]
    for at in range(3):
        for d in range(G):
            cols = pl.ds(pl.multiple_of((g ^ d) * HD, HD), HD)
            outs[at][:, cols] = pieces[at * G + d][...]


def turn_tokens_body(sizes, *refs):
    G, R, count = sizes
    g = lax.axis_index("seq") // R
    for dg in range(G):
        cols = pl.ds(pl.multiple_of((g ^ dg) * HD, HD), HD)
        for dr in range(R):
            refs[G + dr][:, cols] = refs[dg][dr * count : (dr + 1) * count]


def column_body(sizes, *refs):
    G, R, stride = sizes
    for dg in range(G):
        for dr in range(R):
            refs[R + dg][dr * stride : (dr + 1) * stride] = refs[dr][dg * stride : (dg + 1) * stride]


def turn_grads_body(sizes, *refs):
    G, R, stride = sizes
    g = lax.axis_index("seq") // R
    for dg in range(G):
        for dr in range(R):
            at = pl.ds(pl.multiple_of((dr * G + (g ^ dg)) * stride, 16), stride)
            refs[-1][at] = refs[dg][dr * stride : (dr + 1) * stride]


def turn_back_body(sizes, start, arrived, *refs):
    G, R, count = sizes
    g = lax.axis_index("seq") // R
    each = arrived.shape[0] // count
    near, outs = refs[: len(refs) - G * each], refs[len(refs) - G * each :]
    for dg in range(G):
        cols = pl.ds(pl.multiple_of((g ^ dg) * HD, HD), HD)
        for at in range(each):
            total = arrived[at * count : (at + 1) * count, cols].astype(F32)
            for piece in near:
                total = total + piece[start + at * count : start + (at + 1) * count, cols].astype(F32)
            outs[dg * each + at][...] = total.astype(BF16)


def keep_moves(parts, first, shards, full, sems):
    place = lax.axis_index("exp")
    rows, width = shards[0].shape
    moves = []
    for at, shard in enumerate(shards):
        k, h = first + at // parts, at % parts
        cols = pl.ds(pl.multiple_of((place ^ k) * width, 128), width)
        moves.append(pltpu.make_async_copy(shard, full.at[pl.ds(h * rows, rows), cols], sems.at[at]))
    return moves


def through_body(parts, weight, *refs):
    shards, out, full, held, sems, own_sems = refs[:-5], *refs[-5:]
    place = lax.axis_index("exp")
    rows, width = shards[0].shape
    steps = sems.shape[0]
    kept = keep_moves(parts, 0, shards, full, own_sems)
    tall = weight.shape[0] // steps

    def fetch(c):
        mine = pl.ds(c * tall, tall)
        return pltpu.make_async_copy(weight.at[mine], held.at[mine], sems.at[c])

    for c in range(min(2, steps)):
        fetch(c).start()
    for move in kept:
        move.start()
    for c in range(steps):
        fetch(c).wait()
        if c + 2 < steps:
            fetch(c + 2).start()
        for h in range(parts):
            total = None
            for k in range(len(shards) // parts):
                cols = pl.ds(pl.multiple_of((place ^ k) * width, 128), width)
                part = rows_by_rows(shards[k * parts + h][...], held[c * tall : (c + 1) * tall, cols])
                total = part if total is None else total + part
            out[h * rows : (h + 1) * rows, c * tall : (c + 1) * tall] = total
    for move in kept:
        move.wait()


def pre_body(parts, weight, *refs):
    held, sems, own_sems = refs[-3:]
    count = (len(refs) - 7) // (parts + 1)
    shards, refs = refs[: count * parts], refs[count * parts : -3]
    through, full, hidden, hidden_grad, back = *refs[:4], refs[4:]
    place = lax.axis_index("exp")
    rows, width = shards[0].shape
    steps = sems.shape[0]
    wide = weight.shape[1] // steps
    kept = keep_moves(parts, 0, shards, full, own_sems)

    def fetch(c):
        return pltpu.make_async_copy(weight.at[:, pl.ds(c * wide, wide)], held.at[c], sems.at[c])

    for c in range(min(2, steps)):
        fetch(c).start()
    for c in range(steps):
        cols = slice(c * wide, (c + 1) * wide)
        fetch(c).wait()
        if c == 0:
            for move in kept:
                move.start()
        if c + 2 < steps:
            fetch(c + 2).start()
        for h in range(parts):
            mine = slice(h * rows, (h + 1) * rows)
            total = None
            for k in range(len(shards) // parts):
                at = pl.ds(pl.multiple_of((place ^ k) * width, 128), width)
                part = plain(shards[k * parts + h][...], held[c, at, :])
                total = part if total is None else total + part
            logistic = 1.0 / (1.0 + jnp.exp(-total))
            hidden[mine, cols] = (total * logistic).astype(BF16)
            grad = through[mine, cols] * logistic * (1.0 + total * (1.0 - logistic))
            hidden_grad[mine, cols] = grad.astype(BF16)
    for k, out in enumerate(back):
        at = pl.ds(pl.multiple_of((place ^ k) * width, 128), width)
        total = None
        for c in range(steps):
            part = rows_by_rows(hidden_grad[:, c * wide : (c + 1) * wide], held[c, at, :])
            total = part if total is None else total + part
        out[...] = total.astype(out.dtype)
    for move in kept:
        move.wait()


def far_body(kept, moved, *outs):
    rows = outs[0].shape[0]
    for h, out in enumerate(outs):
        mine = slice(h * rows, (h + 1) * rows)
        out[...] = (kept[mine] + moved[mine].astype(F32)).astype(BF16)


def weight_grad_body(place, left, right, out, mark):
    mark[...] = jnp.zeros_like(mark)
    out[...] = cols_by_cols(left[...], right[...]).astype(BF16)


def gather_exp(block, size):
    distance = size // 2
    by_place = {0: block}
    while distance:
        for place in list(by_place):
            by_place[place ^ distance] = swap(by_place[place], "exp", distance)
        distance //= 2
    return [by_place[k] for k in range(size)]


def per_device(
    queries,
    key_rows,
    value_rows,
    out_grad,
    expert_ids,
    gate_values,
    alibi_slope,
    expert_in,
    expert_out,
):
    BL, features = queries.shape
    G = features // HD
    n = lax.axis_size("seq")
    E = lax.axis_size("exp")
    R = n // G
    cap = 5 * BL // (2 * n)
    stride = -(-cap // 16) * 16
    rows = n * stride
    FFL = expert_in.shape[2]
    L = n * BL
    parts = 2
    each = R // parts
    tall = rows // parts
    half = E // 2
    sizes = (G, R, BL, cap, stride)
    limit = attention_limit(BL, L)
    weight_in = expert_in[0]
    weight_out = expert_out[0]

    ids, gates = expert_ids.T, gate_values.T
    arrays_of = lambda arrays: [
        arrays[h * each] if each == 1 else jnp.concatenate(arrays[h * each : (h + 1) * each], axis=0) for h in range(parts)
    ]

    made = local_call(
        functools.partial(pack_body, sizes),
        [((3 * BL + 16, HD), BF16)] * G + [((G * stride, features), BF16)] * R + [((1,), jnp.int32, pltpu.SMEM)],
        [ids, gates],
        far=[queries, key_rows, value_rows, out_grad],
        scratch=[pltpu.VMEM((4, BL, features), BF16), pltpu.SemaphoreType.DMA((4,))],
        limit=57 * MIB,
        nbytes=6 * BL * features * 2,
    )
    place = made[G + R]
    grad_sent = [swap(made[G + dr], "seq", dr) for dr in range(R)]
    own = [swap(made[d], "seq", d * R) for d in range(G)]
    pairs = [
        own[members[0]][: 2 * BL] if len(members) == 1 else jnp.concatenate([own[d][: 2 * BL] for d in members], axis=0)
        for members in pair_groups(G)
    ]
    others = [swap(piece, "seq", dr) for dr in range(1, R) for piece in pairs]
    block = ((16, HD), (3 * BL // 16, 0))
    routing = local_call(
        functools.partial(routing_body, sizes),
        [((G, rows, BL), BF16)],
        [(own[d], *block) for d in range(G)],
        flops=2 * G * 8 * 4 * BL * BL,
        nbytes=rows * BL * G * 2,
    )[0]

    grad_pieces = local_call(
        functools.partial(column_body, (G, R, stride)),
        [((R * stride, features), BF16)] * G,
        grad_sent,
        after=own[1:],
        nbytes=rows * features * 4,
    )
    kept = [((BL, (i + 1) * R * BL), BF16, pltpu.HBM) for i in range(G)]
    kept += [(shape, BF16, pltpu.HBM) for shape in ((G * BL, HD), (L, HD), (L, HD), (G * BL, HD))]
    shapes = kept + [((G * BL, HD), BF16)]
    made = local_call(
        functools.partial(forward_body, sizes),
        shapes,
        own + others,
        scalars=[alibi_slope],
        scratch=[pltpu.VMEM(x[0], x[1]) for x in kept] + [pltpu.SemaphoreType.DMA((G + 4,))],
        flops=0,
        nbytes=0,
        limit=limit,
    )
    probs = list(made[:G])
    attn, keys, values, query_rows = made[G : G + 4]
    grads = local_call(
        functools.partial(turn_grads_body, (G, R, stride)),
        [((rows, features), BF16)],
        [swap(grad_pieces[dg], "seq", dg * R) for dg in range(G)],
        after=[routing, made[G + 4]],
        nbytes=rows * features * 4,
    )[0]
    grads_far = swap(grads, "exp", half)
    token_sent = local_call(
        functools.partial(dispatch_body, sizes),
        [((R * G * stride, HD), BF16)] * G,
        [made[G + 4], routing],
        flops=2 * rows * BL * HD * G,
        nbytes=2 * MIB,
    )
    token_pieces = [swap(token_sent[dg], "seq", dg * R) for dg in range(G)]
    grad_shards = gather_exp(grads, half) + gather_exp(hold([grads_far], token_pieces[1:] or token_pieces)[0], half)
    width = min(256, FFL)
    steps = FFL // width
    whole = lambda array: (array, array.shape, lambda j, p: (0, 0))
    column_of = lambda array: (array, (array.shape[0], width), lambda j, p: (0, j))
    work = 2 * rows * FFL * features
    through, full_grads = local_call(
        functools.partial(through_body, 1),
        [((rows, FFL), F32), ((rows, E * features), BF16, pltpu.HBM)],
        grad_shards,
        far=[weight_out],
        scratch=[
            pltpu.VMEM((FFL, E * features), BF16),
            pltpu.SemaphoreType.DMA((steps,)),
            pltpu.SemaphoreType.DMA((E,)),
        ],
        flops=work * E,
        nbytes=10 * MIB,
    )

    tokens = local_call(
        functools.partial(turn_tokens_body, (G, R, G * stride)),
        [((G * stride, features), BF16)] * R,
        token_pieces,
        after=[grads_far],
        nbytes=rows * features * 4,
    )
    token_parts = arrays_of([swap(tokens[dr], "seq", dr) for dr in range(R)])
    token_parts[1:] = hold(token_parts[1:], [through])
    upper = local_call(
        functools.partial(upper_body, (G, R, BL)),
        [((BL, HD), BF16)] * G,
        [],
        after=token_parts[1:],
        far=[out_grad],
        scratch=[pltpu.SemaphoreType.DMA((G,))],
        nbytes=2 * BL * features * 2,
    )
    upper = [swap(upper[d], "seq", d * R) for d in range(G)]
    far_parts = [swap(part, "exp", half) for part in token_parts]
    if G > 1:
        far_parts[1:] = hold(far_parts[1:], upper[1:])
    near_shards = [gather_exp(part, half) for part in token_parts]
    near_shards = [near_shards[h][k] for k in range(half) for h in range(parts)]
    far_shards = [gather_exp(part, half) for part in far_parts]
    far_shards = [far_shards[h][k] for k in range(half) for h in range(parts)]
    full_tokens, hidden, hidden_grad, *back = local_call(
        functools.partial(pre_body, parts),
        [((rows, E * features), BF16, pltpu.HBM)]
        + [((rows, FFL), BF16)] * 2
        + [((rows, features), BF16 if k % 2 else F32) for k in range(E)],
        near_shards + far_shards + [through],
        far=[weight_in],
        scratch=[
            pltpu.VMEM((steps, E * features, width), BF16),
            pltpu.SemaphoreType.DMA((steps,)),
            pltpu.SemaphoreType.DMA((E * parts,)),
        ],
        flops=2 * work * E,
        nbytes=8 * MIB,
        limit=20 * MIB,
    )

    moved = [swap(back[k], "exp", 1) for k in range(1, E, 2)]
    kept = back[::2]
    pairs = half // 2
    far = [
        local_call(far_body, [((tall, features), BF16)] * parts, [kept[k], moved[k]], nbytes=rows * features * 8)
        for k in range(pairs, 2 * pairs)
    ]
    arrived = [[swap(piece[h], "exp", half) for h in range(parts)] for piece in far]
    near = [[kept[k], moved[k]] for k in range(pairs)]
    distance = half // 2
    while len(near) > 1:
        count = len(near) // 2
        total = [sum(x.astype(F32) for x in near[k]) + jnp.concatenate(arrived[k], axis=0) for k in range(2 * count)]
        sent = [total[count + k].astype(BF16) for k in range(count)]
        arrived = [[swap(x[h * tall : (h + 1) * tall], "exp", distance) for h in range(parts)] for x in sent]
        near = [[x] for x in total[:count]]
        distance //= 2

    mark_out = ((8, 128), F32, (8, 128), lambda j, p: (0, 0))
    out_weight_grad, out_mark = grid_call(
        weight_grad_body,
        steps,
        place,
        [column_of(hidden), whole(full_grads)],
        [((FFL, features * E), BF16, (width, features * E), lambda j, p: (j, 0)), mark_out],
        flops=work * E,
        nbytes=10 * MIB,
    )
    returned = [None] * n
    ready = [out_mark]
    for h in range(parts):
        pieces = local_call(
            functools.partial(turn_back_body, (G, R, G * stride), h * tall),
            [((G * stride, HD), BF16)] * (G * each),
            [arrived[0][h]] + near[0],
            after=ready,
            nbytes=tall * features * 8,
        )
        for dg in range(G):
            for at in range(each):
                d = dg * R + h * each + at
                returned[d] = swap(pieces[dg * each + at], "seq", d)
        ready = returned[R : R + 1]
    in_weight_grad, in_mark = grid_call(
        weight_grad_body,
        E,
        place,
        [(full_tokens, (rows, features), lambda j, p: (0, j)), whole(hidden_grad)],
        [((features * E, FFL), BF16, (features, FFL), lambda j, p: (j, 0)), mark_out],
        flops=work * E,
        nbytes=10 * MIB,
    )

    made = local_call(
        functools.partial(value_body, sizes),
        [((G * BL, HD), BF16)] * (1 + R),
        returned + upper + probs + [routing],
        after=[in_mark],
        scratch=[pltpu.VMEM((L, HD), F32), pltpu.VMEM((G * BL, HD), BF16)],
        flops=2 * G * BL * L * HD,
        nbytes=6 * MIB,
        limit=limit,
    )
    attn_grad, value_parts = made[0], made[1:]
    made = local_call(
        functools.partial(score_body, sizes),
        [((BL, HD), BF16)] * G + [((G * BL, HD), BF16)] * R,
        probs + [attn_grad, attn, keys, values, query_rows],
        scratch=[pltpu.VMEM((G * BL, HD), BF16), pltpu.VMEM((L, HD), F32)],
        flops=6 * G * BL * L * HD,
        nbytes=6 * MIB,
        limit=limit,
    )
    query_pieces, key_parts = made[:G], made[G:]

    def home(pair_parts):
        moved = [swap(pair_parts[dr], "seq", dr) for dr in range(1, R)]
        pieces = []
        for d in range(G):
            mine = slice(d * BL, (d + 1) * BL)
            total = pair_parts[0][mine].astype(F32)
            for piece in moved:
                total = total + piece[mine].astype(F32)
            pieces.append(swap(total.astype(BF16), "seq", d * R))
        return pieces

    value_home = home(value_parts)
    query_home = [swap(query_pieces[d], "seq", d * R) for d in range(G)]
    key_home = home(key_parts)
    query_grad, key_grad, value_grad = local_call(
        functools.partial(unpack_body, (G, R, BL)),
        [((BL, features), BF16)] * 3,
        query_home + key_home + value_home,
        nbytes=6 * BL * features * 2,
    )
    return query_grad, key_grad, value_grad, in_weight_grad[None], out_weight_grad[None]


def solution(mesh):
    return jax.shard_map(
        per_device,
        mesh=mesh,
        in_specs=(
            P("seq", "exp"),
            P("seq", "exp"),
            P("seq", "exp"),
            P("seq", "exp"),
            P("seq", None),
            P("seq", None),
            P("exp"),
            P("seq", None, "exp"),
            P("seq", "exp", None),
        ),
        out_specs=(
            P("seq", "exp"),
            P("seq", "exp"),
            P("seq", "exp"),
            P("seq", None, "exp"),
            P("seq", "exp", None),
        ),
        check_vma=False,
    )
```

```python
import functools
import math

import jax
import jax.numpy as jnp
from jax import lax
from jax.experimental import pallas as pl
from jax.experimental.pallas import tpu as pltpu
from jax.sharding import PartitionSpec as P

HD = 128
WCH = 16
LOG2E = math.log2(math.e)
BF16 = jnp.bfloat16
F32 = jnp.float32
MIB = 1024 * 1024
VMEM_LIMIT = 14 * MIB


def on(pair, dims):
    return lax.dot_general(pair[0], pair[1], ((dims[0], dims[1]), ((), ())), preferred_element_type=F32)


def rows_by_rows(a, b):
    return on((a, b), ((1,), (1,)))


def cols_by_cols(a, b):
    return on((a, b), ((0,), (0,)))


def plain(a, b):
    return on((a, b), ((1,), (0,)))


def swap(block, axis, distance):
    if distance == 0:
        return block
    devices = range(lax.axis_size(axis))
    return lax.ppermute(block, axis, [(i, i ^ distance) for i in devices])


def local_call(body, out_shapes, arrays, scalars=(), after=(), far=(), into=(), aliases=None, scratch=(), flops=0, nbytes=0, limit=VMEM_LIMIT):
    smem = pl.BlockSpec(memory_space=pltpu.SMEM)
    vmem = pl.BlockSpec(memory_space=pltpu.VMEM)
    anywhere = pl.BlockSpec(memory_space=pl.ANY)
    hbm = pl.BlockSpec(memory_space=pltpu.HBM)
    lead = len(scalars)
    grid = (1,) if any(isinstance(x, tuple) for x in arrays) else ()
    specs = [pl.BlockSpec(x[1], lambda j, at=x[2]: at) if isinstance(x, tuple) else vmem for x in arrays] + [hbm] * len(into)
    arrays = [x[0] if isinstance(x, tuple) else x for x in arrays]

    def kernel(*refs):
        body(*refs[:lead], *refs[lead + len(after) :])

    return pl.pallas_call(
        kernel,
        out_shape=[jax.ShapeDtypeStruct(x[0], x[1]) for x in out_shapes],
        grid=grid,
        in_specs=[smem] * lead + [anywhere] * len(after) + [hbm] * len(far) + specs,
        out_specs=[pl.BlockSpec(memory_space=x[2]) if len(x) > 2 else vmem for x in out_shapes],
        scratch_shapes=list(scratch),
        input_output_aliases=aliases or {},
        compiler_params=pltpu.CompilerParams(vmem_limit_bytes=limit),
        cost_estimate=pl.CostEstimate(flops=flops, bytes_accessed=nbytes, transcendentals=0),
    )(*scalars, *after, *far, *arrays, *into)


def hold(arrays, after):
    def body(*refs):
        pass

    anywhere = pl.BlockSpec(memory_space=pl.ANY)
    lead = len(after)
    return list(
        pl.pallas_call(
            body,
            out_shape=[jax.ShapeDtypeStruct(x.shape, x.dtype) for x in arrays],
            in_specs=[anywhere] * (lead + len(arrays)),
            out_specs=[anywhere] * len(arrays),
            input_output_aliases={lead + at: at for at in range(len(arrays))},
            compiler_params=pltpu.CompilerParams(vmem_limit_bytes=MIB),
        )(*after, *arrays)
    )


def grid_call(body, steps, exp_index, ins, outs, after=(), flops=0, nbytes=0, limit=VMEM_LIMIT):
    anywhere = pl.BlockSpec(memory_space=pl.ANY)

    def kernel(place, *refs):
        body(place[0], *refs[len(after) :])

    return pl.pallas_call(
        kernel,
        out_shape=[jax.ShapeDtypeStruct(shape, dtype) for shape, dtype, _, _ in outs],
        grid_spec=pltpu.PrefetchScalarGridSpec(
            num_scalar_prefetch=1,
            grid=(steps,),
            in_specs=[anywhere] * len(after) + [pl.BlockSpec(block, index) for _, block, index in ins],
            out_specs=[pl.BlockSpec(block, index) for _, _, block, index in outs],
        ),
        compiler_params=pltpu.CompilerParams(vmem_limit_bytes=limit),
        cost_estimate=pl.CostEstimate(flops=flops, bytes_accessed=nbytes, transcendentals=0),
    )(exp_index, *after, *[array for array, _, _ in ins])


def attention_limit(block_len, total):
    return min(60 * MIB, 4 * MIB + 6 * block_len * total * 4)


def id_rows_of(ids):
    return [ids[j : j + 1, at : at + 128].astype(F32) for j in range(2) for at in range(0, ids.shape[1], 128)]


def relative_slots(id_rows, place, experts, capacity, stride):
    flat = jnp.concatenate(id_rows, axis=1).astype(jnp.int32)
    entries = flat.shape[1]
    lanes = max(experts, 8)
    one_hot = lax.broadcasted_iota(jnp.int32, (lanes, entries), 0) == flat
    one_hot = one_hot.astype(F32)
    earlier = lax.broadcasted_iota(jnp.int32, (entries, entries), 0) < lax.broadcasted_iota(
        jnp.int32, (entries, entries), 1
    )
    before = plain(one_hot.astype(BF16), earlier.astype(F32).astype(BF16))
    position = jnp.sum(before * one_hot, axis=0, keepdims=True).astype(jnp.int32)
    return jnp.where(position < capacity, (flat ^ place) * stride + position, -1)


def pack_body(sizes, q, k, v, og, ids, gates, *refs):
    G, R, BL = sizes[:3]
    outs, sent, place, held, sems = refs[:G], refs[G : G + R], *refs[G + R :]
    g = lax.axis_index("seq") // R
    place[0] = lax.axis_index("exp")

    moves = [pltpu.make_async_copy(source, held.at[at], sems.at[at]) for at, source in enumerate((k, v, q, og))]
    for move in moves:
        move.start()
    rows = id_rows_of(ids)
    rows.append(jnp.zeros((16 - len(rows), 128), F32))
    rows = jnp.concatenate(rows, axis=0).astype(BF16)
    for d in range(G):
        outs[d][3 * BL : 3 * BL + 16] = rows
    for at, move in enumerate(moves[:3]):
        move.wait()
        for d in range(G):
            cols = pl.ds(pl.multiple_of((g ^ d) * HD, HD), HD)
            outs[d][at * BL : (at + 1) * BL] = held[at, :, cols]
    moves[3].wait()
    route_grads(sizes, held[3], gates, ids, sent)


def upper_body(sizes, og, *refs):
    G, R, BL = sizes
    outs, sems = refs[:G], refs[G]
    g = lax.axis_index("seq") // R
    moves = []
    for d in range(G):
        cols = pl.ds(pl.multiple_of((g ^ d) * HD, HD), HD)
        moves.append(pltpu.make_async_copy(og.at[:, cols], outs[d], sems.at[d]))
    for move in moves:
        move.start()
    for move in moves:
        move.wait()


def route_grads(sizes, block, gates, ids, outs):
    G, R, BL, cap, stride = sizes
    n = G * R
    slots = relative_slots(id_rows_of(ids), lax.axis_index("seq"), n, cap, stride)
    routing = lax.broadcasted_iota(jnp.int32, (n * stride, 2 * BL), 0) == slots
    diagonal = lax.broadcasted_iota(jnp.int32, (BL, BL), 0) == lax.broadcasted_iota(jnp.int32, (BL, BL), 1)
    block = block.astype(F32)
    scaled = []
    for j in range(2):
        gate = jnp.sum(jnp.where(diagonal, gates[j : j + 1], 0.0), axis=1, keepdims=True)
        scaled.append((gate * block).astype(BF16))
    routed = plain(routing.astype(F32).astype(BF16), jnp.concatenate(scaled, axis=0)).astype(BF16)
    for dg in range(G):
        for dr in range(R):
            d = dg * R + dr
            outs[dr][dg * stride : (dg + 1) * stride] = routed[d * stride : (d + 1) * stride]


def routing_body(sizes, *refs):
    G, R, BL, cap, stride = sizes
    n = G * R
    s = lax.axis_index("seq")
    own, out = refs[:G], refs[G]
    for d in range(G):
        rows = own[d][...].astype(F32)
        slots = relative_slots([rows[k : k + 1] for k in range(2 * BL // 128)], s, n, cap, stride)
        slot_rows = lax.broadcasted_iota(jnp.int32, (n * stride, BL), 0)
        chosen = (slot_rows == slots[:, :BL]) | (slot_rows == slots[:, BL:])
        out[pl.ds((s // R) ^ d, 1)] = chosen.astype(F32).astype(BF16)[None]


def pair_groups(G):
    return [members for members in ([0], list(range(1, G))) if members and members[-1] < G]


def forward_body(sizes, slopes, *refs):
    G, R, BL, cap, stride = sizes
    n = G * R
    total = n * BL
    s = lax.axis_index("seq")
    g, r = s // R, s % R
    own, refs = refs[:G], refs[G:]
    groups = pair_groups(G)
    others, refs = refs[: len(groups) * (R - 1)], refs[len(groups) * (R - 1) :]
    far, refs = refs[: G + 4], refs[G + 4 :]
    attn_out, refs = refs[0], refs[1:]
    near, sems = refs[: G + 4], refs[G + 4]
    probs = near[:G]
    attn, keys, values, queries = near[G:]

    def kept(at):
        return pltpu.make_async_copy(near[at], far[at], sems.at[at])

    for d in range(G):
        i = g ^ d
        queries[pl.ds(pl.multiple_of(i * BL, BL), BL)] = own[d][2 * BL : 3 * BL]
        for dr in range(R):
            piece, at = own[d], 0
            if dr:
                group = next(k for k, members in enumerate(groups) if d in members)
                piece = others[(dr - 1) * len(groups) + group]
                at = groups[group].index(d) * 2 * BL
            rows = pl.ds(pl.multiple_of((i * R + (r ^ dr)) * BL, BL), BL)
            keys[rows] = piece[at : at + BL]
            values[rows] = piece[at + BL : at + 2 * BL]
    for at in range(G + 1, G + 4):
        kept(at).start()
    slope = slopes[g]
    span = R * BL
    for i in range(G):
        N = (i + 1) * span
        scores = rows_by_rows(queries[i * BL : (i + 1) * BL], keys[0:N])
        col = lax.broadcasted_iota(jnp.int32, (1, N), 1)
        bias = (col - N).astype(F32) * (slope * LOG2E)
        scores = scores * (HD**-0.5 * LOG2E) + bias
        if total > WCH * BL:
            distance = (
                lax.broadcasted_iota(jnp.int32, (BL, N), 0) + (i * R + r) * BL - lax.broadcasted_iota(jnp.int32, (BL, N), 1)
            )
            scores = jnp.where((distance >= 0) & (distance < WCH * BL), scores, -jnp.inf)
        else:
            ahead = lax.broadcasted_iota(jnp.int32, (BL, span), 1) - lax.broadcasted_iota(jnp.int32, (BL, span), 0)
            last = jnp.where(ahead <= r * BL, scores[:, N - span :], -jnp.inf)
            scores = last if i == 0 else jnp.concatenate([scores[:, : N - span], last], axis=1)
        top = jnp.max(scores, axis=1, keepdims=True)
        grown = jnp.exp2(scores - top)
        norm = jnp.sum(grown, axis=1, keepdims=True)
        weights = (grown * (1.0 / norm)).astype(BF16)
        probs[i][...] = weights
        kept(i).start()
        out = plain(weights, values[0:N]).astype(BF16)
        attn[i * BL : (i + 1) * BL] = out
        attn_out[i * BL : (i + 1) * BL] = out
    kept(G).start()
    for at in range(G + 4):
        kept(at).wait()


def dispatch_body(sizes, attn, routing, *sent):
    G, R, BL, cap, stride = sizes
    for i in range(G):
        routed = plain(routing[i], attn[i * BL : (i + 1) * BL]).astype(BF16)
        for dg in range(G):
            for dr in range(R):
                d = dg * R + dr
                at = (dr * G + i) * stride
                sent[dg][at : at + stride] = routed[d * stride : (d + 1) * stride]


def spread(sizes, total, outs):
    G, R, BL = sizes[:3]
    s = lax.axis_index("seq")
    g, r = s // R, s % R
    for d in range(G):
        for dr in range(R):
            rows = pl.ds(pl.multiple_of(((g ^ d) * R + (r ^ dr)) * BL, BL), BL)
            outs[dr][d * BL : (d + 1) * BL] = total[rows].astype(BF16)


def backward_body(sizes, *refs):
    G, R, BL, cap, stride = sizes
    n = G * R
    g = lax.axis_index("seq") // R
    back, refs = refs[:n], refs[n:]
    upper, refs = refs[:G], refs[G:]
    probs, refs = refs[:G], refs[G:]
    routing, attn, keys, values, queries, refs = *refs[:5], refs[5:]
    query_out, refs = refs[:G], refs[G:]
    value_out, key_out, refs = refs[:R], refs[R : 2 * R], refs[2 * R :]
    upper_rows, query_rows, value_sum, key_sum = refs
    scale = HD**-0.5
    for d in range(G):
        upper_rows[pl.ds(pl.multiple_of((g ^ d) * BL, BL), BL)] = upper[d][...]
    for i in reversed(range(G)):
        N = (i + 1) * R * BL
        mine = slice(i * BL, (i + 1) * BL)
        rows = jnp.concatenate([back[d][i * stride : (i + 1) * stride] for d in range(n)], axis=0)
        picked = cols_by_cols(routing[i], rows)
        grad = (upper_rows[mine].astype(F32) + picked).astype(BF16)
        weights = probs[i][...]
        value_part = cols_by_cols(weights, grad)
        delta = jnp.sum(grad.astype(F32) * attn[mine].astype(F32), axis=1, keepdims=True)
        dprob = rows_by_rows(grad, values[0:N])
        dscore = (weights.astype(F32) * (dprob - delta)).astype(BF16)
        query_rows[mine] = (plain(dscore, keys[0:N]) * scale).astype(BF16)
        key_part = cols_by_cols(dscore, queries[mine]) * scale
        if i == G - 1:
            value_sum[...] = value_part
            key_sum[...] = key_part
        else:
            value_sum[0:N] += value_part
            key_sum[0:N] += key_part
    for d in range(G):
        query_out[d][...] = query_rows[pl.ds(pl.multiple_of((g ^ d) * BL, BL), BL)]
    spread(sizes, value_sum, value_out)
    spread(sizes, key_sum, key_out)


def unpack_body(sizes, *refs):
    G, R, BL = sizes
    g = lax.axis_index("seq") // R
    pieces, outs = refs[: 3 * G], refs[3 * G :]
    for at in range(3):
        for d in range(G):
            cols = pl.ds(pl.multiple_of((g ^ d) * HD, HD), HD)
            outs[at][:, cols] = pieces[at * G + d][...]


def turn_tokens_body(sizes, *refs):
    G, R, count = sizes
    g = lax.axis_index("seq") // R
    for dg in range(G):
        cols = pl.ds(pl.multiple_of((g ^ dg) * HD, HD), HD)
        for dr in range(R):
            refs[G + dr][:, cols] = refs[dg][dr * count : (dr + 1) * count]


def column_body(sizes, *refs):
    G, R, stride = sizes
    for dg in range(G):
        for dr in range(R):
            refs[R + dg][dr * stride : (dr + 1) * stride] = refs[dr][dg * stride : (dg + 1) * stride]


def turn_grads_body(sizes, *refs):
    G, R, stride = sizes
    g = lax.axis_index("seq") // R
    for dg in range(G):
        for dr in range(R):
            at = pl.ds(pl.multiple_of((dr * G + (g ^ dg)) * stride, 16), stride)
            refs[-1][at] = refs[dg][dr * stride : (dr + 1) * stride]


def turn_back_body(sizes, start, arrived, *refs):
    G, R, count = sizes
    g = lax.axis_index("seq") // R
    each = arrived.shape[0] // count
    near, outs = refs[: len(refs) - G * each], refs[len(refs) - G * each :]
    for dg in range(G):
        cols = pl.ds(pl.multiple_of((g ^ dg) * HD, HD), HD)
        for at in range(each):
            total = arrived[at * count : (at + 1) * count, cols].astype(F32)
            for piece in near:
                total = total + piece[start + at * count : start + (at + 1) * count, cols].astype(F32)
            outs[dg * each + at][...] = total.astype(BF16)


def keep_moves(parts, first, shards, full, sems):
    place = lax.axis_index("exp")
    rows, width = shards[0].shape
    moves = []
    for at, shard in enumerate(shards):
        k, h = first + at // parts, at % parts
        cols = pl.ds(pl.multiple_of((place ^ k) * width, 128), width)
        moves.append(pltpu.make_async_copy(shard, full.at[pl.ds(h * rows, rows), cols], sems.at[at]))
    return moves


def through_body(parts, weight, *refs):
    shards, out, full, held, sems, own_sems = refs[:-5], *refs[-5:]
    place = lax.axis_index("exp")
    rows, width = shards[0].shape
    steps = sems.shape[0]
    kept = keep_moves(parts, 0, shards, full, own_sems)
    tall = weight.shape[0] // steps

    def fetch(c):
        mine = pl.ds(c * tall, tall)
        return pltpu.make_async_copy(weight.at[mine], held.at[mine], sems.at[c])

    for c in range(min(2, steps)):
        fetch(c).start()
    for move in kept:
        move.start()
    for c in range(steps):
        fetch(c).wait()
        if c + 2 < steps:
            fetch(c + 2).start()
        for h in range(parts):
            total = None
            for k in range(len(shards) // parts):
                cols = pl.ds(pl.multiple_of((place ^ k) * width, 128), width)
                part = rows_by_rows(shards[k * parts + h][...], held[c * tall : (c + 1) * tall, cols])
                total = part if total is None else total + part
            out[h * rows : (h + 1) * rows, c * tall : (c + 1) * tall] = total
    for move in kept:
        move.wait()


def pre_body(parts, weight, *refs):
    held, sems, own_sems = refs[-3:]
    count = (len(refs) - 7) // (parts + 1)
    shards, refs = refs[: count * parts], refs[count * parts : -3]
    through, full, hidden, hidden_grad, back = *refs[:4], refs[4:]
    place = lax.axis_index("exp")
    rows, width = shards[0].shape
    steps = sems.shape[0]
    wide = weight.shape[1] // steps
    kept = keep_moves(parts, 0, shards, full, own_sems)

    def fetch(c):
        return pltpu.make_async_copy(weight.at[:, pl.ds(c * wide, wide)], held.at[c], sems.at[c])

    for c in range(min(2, steps)):
        fetch(c).start()
    for c in range(steps):
        cols = slice(c * wide, (c + 1) * wide)
        fetch(c).wait()
        if c == 0:
            for move in kept:
                move.start()
        if c + 2 < steps:
            fetch(c + 2).start()
        for h in range(parts):
            mine = slice(h * rows, (h + 1) * rows)
            total = None
            for k in range(len(shards) // parts):
                at = pl.ds(pl.multiple_of((place ^ k) * width, 128), width)
                part = plain(shards[k * parts + h][...], held[c, at, :])
                total = part if total is None else total + part
            logistic = 1.0 / (1.0 + jnp.exp(-total))
            hidden[mine, cols] = (total * logistic).astype(BF16)
            grad = through[mine, cols] * logistic * (1.0 + total * (1.0 - logistic))
            hidden_grad[mine, cols] = grad.astype(BF16)
    for k, out in enumerate(back):
        at = pl.ds(pl.multiple_of((place ^ k) * width, 128), width)
        total = None
        for c in range(steps):
            part = rows_by_rows(hidden_grad[:, c * wide : (c + 1) * wide], held[c, at, :])
            total = part if total is None else total + part
        out[...] = total.astype(out.dtype)
    for move in kept:
        move.wait()


def far_body(kept, moved, *outs):
    rows = outs[0].shape[0]
    for h, out in enumerate(outs):
        mine = slice(h * rows, (h + 1) * rows)
        out[...] = (kept[mine] + moved[mine].astype(F32)).astype(BF16)


def weight_grad_body(place, left, right, out, mark):
    mark[...] = jnp.zeros_like(mark)
    out[...] = cols_by_cols(left[...], right[...]).astype(BF16)


def gather_exp(block, size):
    distance = size // 2
    by_place = {0: block}
    while distance:
        for place in list(by_place):
            by_place[place ^ distance] = swap(by_place[place], "exp", distance)
        distance //= 2
    return [by_place[k] for k in range(size)]


def per_device(
    queries,
    key_rows,
    value_rows,
    out_grad,
    expert_ids,
    gate_values,
    alibi_slope,
    expert_in,
    expert_out,
):
    BL, features = queries.shape
    G = features // HD
    n = lax.axis_size("seq")
    E = lax.axis_size("exp")
    R = n // G
    cap = 5 * BL // (2 * n)
    stride = -(-cap // 16) * 16
    rows = n * stride
    FFL = expert_in.shape[2]
    L = n * BL
    parts = 2
    each = R // parts
    tall = rows // parts
    half = E // 2
    sizes = (G, R, BL, cap, stride)
    limit = attention_limit(BL, L)
    weight_in = expert_in[0]
    weight_out = expert_out[0]

    ids, gates = expert_ids.T, gate_values.T
    arrays_of = lambda arrays: [
        arrays[h * each] if each == 1 else jnp.concatenate(arrays[h * each : (h + 1) * each], axis=0) for h in range(parts)
    ]

    made = local_call(
        functools.partial(pack_body, sizes),
        [((3 * BL + 16, HD), BF16)] * G + [((G * stride, features), BF16)] * R + [((1,), jnp.int32, pltpu.SMEM)],
        [ids, gates],
        far=[queries, key_rows, value_rows, out_grad],
        scratch=[pltpu.VMEM((4, BL, features), BF16), pltpu.SemaphoreType.DMA((4,))],
        limit=57 * MIB,
        nbytes=6 * BL * features * 2,
    )
    place = made[G + R]
    grad_sent = [swap(made[G + dr], "seq", dr) for dr in range(R)]
    own = [swap(made[d], "seq", d * R) for d in range(G)]
    pairs = [
        own[members[0]][: 2 * BL] if len(members) == 1 else jnp.concatenate([own[d][: 2 * BL] for d in members], axis=0)
        for members in pair_groups(G)
    ]
    others = [swap(piece, "seq", dr) for dr in range(1, R) for piece in pairs]
    block = ((16, HD), (3 * BL // 16, 0))
    routing = local_call(
        functools.partial(routing_body, sizes),
        [((G, rows, BL), BF16)],
        [(own[d], *block) for d in range(G)],
        flops=2 * G * 8 * 4 * BL * BL,
        nbytes=rows * BL * G * 2,
    )[0]

    grad_pieces = local_call(
        functools.partial(column_body, (G, R, stride)),
        [((R * stride, features), BF16)] * G,
        grad_sent,
        after=own[1:],
        nbytes=rows * features * 4,
    )
    kept = [((BL, (i + 1) * R * BL), BF16, pltpu.HBM) for i in range(G)]
    kept += [(shape, BF16, pltpu.HBM) for shape in ((G * BL, HD), (L, HD), (L, HD), (G * BL, HD))]
    shapes = kept + [((G * BL, HD), BF16)]
    made = local_call(
        functools.partial(forward_body, sizes),
        shapes,
        own + others,
        scalars=[alibi_slope],
        scratch=[pltpu.VMEM(x[0], x[1]) for x in kept] + [pltpu.SemaphoreType.DMA((G + 4,))],
        flops=0,
        nbytes=0,
        limit=limit,
    )
    probs = list(made[:G])
    attn, keys, values, query_rows = made[G : G + 4]
    token_sent = local_call(
        functools.partial(dispatch_body, sizes),
        [((R * G * stride, HD), BF16)] * G,
        [made[G + 4], routing],
        flops=2 * rows * BL * HD * G,
        nbytes=2 * MIB,
    )
    grads = local_call(
        functools.partial(turn_grads_body, (G, R, stride)),
        [((rows, features), BF16)],
        [swap(grad_pieces[dg], "seq", dg * R) for dg in range(G)],
        after=token_sent[:1],
        nbytes=rows * features * 4,
    )[0]
    grads_far = swap(grads, "exp", half)
    token_pieces = [swap(token_sent[dg], "seq", dg * R) for dg in range(G)]
    grad_shards = gather_exp(grads, half) + gather_exp(hold([grads_far], token_pieces[1:] or token_pieces)[0], half)
    width = min(256, FFL)
    steps = FFL // width
    whole = lambda array: (array, array.shape, lambda j, p: (0, 0))
    column_of = lambda array: (array, (array.shape[0], width), lambda j, p: (0, j))
    work = 2 * rows * FFL * features
    through, full_grads = local_call(
        functools.partial(through_body, 1),
        [((rows, FFL), F32), ((rows, E * features), BF16, pltpu.HBM)],
        grad_shards,
        far=[weight_out],
        scratch=[
            pltpu.VMEM((FFL, E * features), BF16),
            pltpu.SemaphoreType.DMA((steps,)),
            pltpu.SemaphoreType.DMA((E,)),
        ],
        flops=work * E,
        nbytes=10 * MIB,
    )

    tokens = local_call(
        functools.partial(turn_tokens_body, (G, R, G * stride)),
        [((G * stride, features), BF16)] * R,
        token_pieces,
        after=[grads_far],
        nbytes=rows * features * 4,
    )
    token_parts = arrays_of([swap(tokens[dr], "seq", dr) for dr in range(R)])
    token_parts[1:] = hold(token_parts[1:], [through])
    upper = local_call(
        functools.partial(upper_body, (G, R, BL)),
        [((BL, HD), BF16)] * G,
        [],
        after=token_parts[1:],
        far=[out_grad],
        scratch=[pltpu.SemaphoreType.DMA((G,))],
        nbytes=2 * BL * features * 2,
    )
    upper = [swap(upper[d], "seq", d * R) for d in range(G)]
    far_parts = [swap(part, "exp", half) for part in token_parts]
    if G > 1:
        far_parts[1:] = hold(far_parts[1:], upper[1:])
    near_shards = [gather_exp(part, half) for part in token_parts]
    near_shards = [near_shards[h][k] for k in range(half) for h in range(parts)]
    far_shards = [gather_exp(part, half) for part in far_parts]
    far_shards = [far_shards[h][k] for k in range(half) for h in range(parts)]
    full_tokens, hidden, hidden_grad, *back = local_call(
        functools.partial(pre_body, parts),
        [((rows, E * features), BF16, pltpu.HBM)]
        + [((rows, FFL), BF16)] * 2
        + [((rows, features), BF16 if k % 2 else F32) for k in range(E)],
        near_shards + far_shards + [through],
        far=[weight_in],
        scratch=[
            pltpu.VMEM((steps, E * features, width), BF16),
            pltpu.SemaphoreType.DMA((steps,)),
            pltpu.SemaphoreType.DMA((E * parts,)),
        ],
        flops=2 * work * E,
        nbytes=8 * MIB,
        limit=20 * MIB,
    )

    moved = [swap(back[k], "exp", 1) for k in range(1, E, 2)]
    kept = back[::2]
    pairs = half // 2
    far = [
        local_call(far_body, [((tall, features), BF16)] * parts, [kept[k], moved[k]], nbytes=rows * features * 8)
        for k in range(pairs, 2 * pairs)
    ]
    arrived = [[swap(piece[h], "exp", half) for h in range(parts)] for piece in far]
    near = [[kept[k], moved[k]] for k in range(pairs)]
    distance = half // 2
    while len(near) > 1:
        count = len(near) // 2
        total = [sum(x.astype(F32) for x in near[k]) + jnp.concatenate(arrived[k], axis=0) for k in range(2 * count)]
        sent = [total[count + k].astype(BF16) for k in range(count)]
        arrived = [[swap(x[h * tall : (h + 1) * tall], "exp", distance) for h in range(parts)] for x in sent]
        near = [[x] for x in total[:count]]
        distance //= 2

    mark_out = ((8, 128), F32, (8, 128), lambda j, p: (0, 0))
    out_weight_grad, out_mark = grid_call(
        weight_grad_body,
        steps,
        place,
        [column_of(hidden), whole(full_grads)],
        [((FFL, features * E), BF16, (width, features * E), lambda j, p: (j, 0)), mark_out],
        flops=work * E,
        nbytes=10 * MIB,
    )
    returned = [None] * n
    ready = [out_mark]
    for h in range(parts):
        pieces = local_call(
            functools.partial(turn_back_body, (G, R, G * stride), h * tall),
            [((G * stride, HD), BF16)] * (G * each),
            [arrived[0][h]] + near[0],
            after=ready,
            nbytes=tall * features * 8,
        )
        for dg in range(G):
            for at in range(each):
                d = dg * R + h * each + at
                returned[d] = swap(pieces[dg * each + at], "seq", d)
        ready = returned[R : R + 1]
    in_weight_grad, in_mark = grid_call(
        weight_grad_body,
        E,
        place,
        [(full_tokens, (rows, features), lambda j, p: (0, j)), whole(hidden_grad)],
        [((features * E, FFL), BF16, (features, FFL), lambda j, p: (j, 0)), mark_out],
        flops=work * E,
        nbytes=10 * MIB,
    )

    made = local_call(
        functools.partial(backward_body, sizes),
        [((BL, HD), BF16)] * G + [((G * BL, HD), BF16)] * (2 * R),
        returned + upper + probs + [routing, attn, keys, values, query_rows],
        after=[in_mark],
        scratch=[
            pltpu.VMEM((G * BL, HD), BF16),
            pltpu.VMEM((G * BL, HD), BF16),
            pltpu.VMEM((L, HD), F32),
            pltpu.VMEM((L, HD), F32),
        ],
        flops=8 * G * BL * L * HD,
        nbytes=10 * MIB,
        limit=limit,
    )
    query_pieces, value_parts, key_parts = made[:G], made[G : G + R], made[G + R :]

    def home(pair_parts):
        moved = [swap(pair_parts[dr], "seq", dr) for dr in range(1, R)]
        pieces = []
        for d in range(G):
            mine = slice(d * BL, (d + 1) * BL)
            total = pair_parts[0][mine].astype(F32)
            for piece in moved:
                total = total + piece[mine].astype(F32)
            pieces.append(swap(total.astype(BF16), "seq", d * R))
        return pieces

    value_home = home(value_parts)
    query_home = [swap(query_pieces[d], "seq", d * R) for d in range(G)]
    key_home = home(key_parts)
    query_grad, key_grad, value_grad = local_call(
        functools.partial(unpack_body, (G, R, BL)),
        [((BL, features), BF16)] * 3,
        query_home + key_home + value_home,
        nbytes=6 * BL * features * 2,
    )
    return query_grad, key_grad, value_grad, in_weight_grad[None], out_weight_grad[None]


def solution(mesh):
    return jax.shard_map(
        per_device,
        mesh=mesh,
        in_specs=(
            P("seq", "exp"),
            P("seq", "exp"),
            P("seq", "exp"),
            P("seq", "exp"),
            P("seq", None),
            P("seq", None),
            P("exp"),
            P("seq", None, "exp"),
            P("seq", "exp", None),
        ),
        out_specs=(
            P("seq", "exp"),
            P("seq", "exp"),
            P("seq", "exp"),
            P("seq", None, "exp"),
            P("seq", "exp", None),
        ),
        check_vma=False,
    )
```

```python
import functools
import math

import jax
import jax.numpy as jnp
from jax import lax
from jax.experimental import pallas as pl
from jax.experimental.pallas import tpu as pltpu
from jax.sharding import PartitionSpec as P

HD = 128
WCH = 16
LOG2E = math.log2(math.e)
BF16 = jnp.bfloat16
F32 = jnp.float32
MIB = 1024 * 1024
VMEM_LIMIT = 14 * MIB


def on(pair, dims):
    return lax.dot_general(pair[0], pair[1], ((dims[0], dims[1]), ((), ())), preferred_element_type=F32)


def rows_by_rows(a, b):
    return on((a, b), ((1,), (1,)))


def cols_by_cols(a, b):
    return on((a, b), ((0,), (0,)))


def plain(a, b):
    return on((a, b), ((1,), (0,)))


def swap(block, axis, distance):
    if distance == 0:
        return block
    devices = range(lax.axis_size(axis))
    return lax.ppermute(block, axis, [(i, i ^ distance) for i in devices])


def local_call(body, out_shapes, arrays, scalars=(), after=(), far=(), into=(), aliases=None, scratch=(), flops=0, nbytes=0, limit=VMEM_LIMIT):
    smem = pl.BlockSpec(memory_space=pltpu.SMEM)
    vmem = pl.BlockSpec(memory_space=pltpu.VMEM)
    anywhere = pl.BlockSpec(memory_space=pl.ANY)
    hbm = pl.BlockSpec(memory_space=pltpu.HBM)
    lead = len(scalars)
    grid = (1,) if any(isinstance(x, tuple) for x in arrays) else ()
    specs = [pl.BlockSpec(x[1], lambda j, at=x[2]: at) if isinstance(x, tuple) else vmem for x in arrays] + [hbm] * len(into)
    arrays = [x[0] if isinstance(x, tuple) else x for x in arrays]

    def kernel(*refs):
        body(*refs[:lead], *refs[lead + len(after) :])

    return pl.pallas_call(
        kernel,
        out_shape=[jax.ShapeDtypeStruct(x[0], x[1]) for x in out_shapes],
        grid=grid,
        in_specs=[smem] * lead + [anywhere] * len(after) + [hbm] * len(far) + specs,
        out_specs=[pl.BlockSpec(memory_space=x[2]) if len(x) > 2 else vmem for x in out_shapes],
        scratch_shapes=list(scratch),
        input_output_aliases=aliases or {},
        compiler_params=pltpu.CompilerParams(vmem_limit_bytes=limit),
        cost_estimate=pl.CostEstimate(flops=flops, bytes_accessed=nbytes, transcendentals=0),
    )(*scalars, *after, *far, *arrays, *into)


def hold(arrays, after):
    def body(*refs):
        pass

    anywhere = pl.BlockSpec(memory_space=pl.ANY)
    lead = len(after)
    return list(
        pl.pallas_call(
            body,
            out_shape=[jax.ShapeDtypeStruct(x.shape, x.dtype) for x in arrays],
            in_specs=[anywhere] * (lead + len(arrays)),
            out_specs=[anywhere] * len(arrays),
            input_output_aliases={lead + at: at for at in range(len(arrays))},
            compiler_params=pltpu.CompilerParams(vmem_limit_bytes=MIB),
        )(*after, *arrays)
    )


def grid_call(body, steps, exp_index, ins, outs, after=(), flops=0, nbytes=0, limit=VMEM_LIMIT):
    anywhere = pl.BlockSpec(memory_space=pl.ANY)

    def kernel(place, *refs):
        body(place[0], *refs[len(after) :])

    return pl.pallas_call(
        kernel,
        out_shape=[jax.ShapeDtypeStruct(shape, dtype) for shape, dtype, _, _ in outs],
        grid_spec=pltpu.PrefetchScalarGridSpec(
            num_scalar_prefetch=1,
            grid=(steps,),
            in_specs=[anywhere] * len(after) + [pl.BlockSpec(block, index) for _, block, index in ins],
            out_specs=[pl.BlockSpec(block, index) for _, _, block, index in outs],
        ),
        compiler_params=pltpu.CompilerParams(vmem_limit_bytes=limit),
        cost_estimate=pl.CostEstimate(flops=flops, bytes_accessed=nbytes, transcendentals=0),
    )(exp_index, *after, *[array for array, _, _ in ins])


def attention_limit(block_len, total):
    return min(60 * MIB, 4 * MIB + 6 * block_len * total * 4)


def id_rows_of(ids):
    return [ids[j : j + 1, at : at + 128].astype(F32) for j in range(2) for at in range(0, ids.shape[1], 128)]


def relative_slots(id_rows, place, experts, capacity, stride):
    flat = jnp.concatenate(id_rows, axis=1).astype(jnp.int32)
    entries = flat.shape[1]
    lanes = max(experts, 8)
    one_hot = lax.broadcasted_iota(jnp.int32, (lanes, entries), 0) == flat
    one_hot = one_hot.astype(F32)
    earlier = lax.broadcasted_iota(jnp.int32, (entries, entries), 0) < lax.broadcasted_iota(
        jnp.int32, (entries, entries), 1
    )
    before = plain(one_hot.astype(BF16), earlier.astype(F32).astype(BF16))
    position = jnp.sum(before * one_hot, axis=0, keepdims=True).astype(jnp.int32)
    return jnp.where(position < capacity, (flat ^ place) * stride + position, -1)


def pack_body(sizes, q, k, v, og, ids, gates, *refs):
    G, R, BL = sizes[:3]
    outs, sent, place, held, sems = refs[:G], refs[G : G + R], *refs[G + R :]
    g = lax.axis_index("seq") // R
    place[0] = lax.axis_index("exp")

    moves = [pltpu.make_async_copy(source, held.at[at], sems.at[at]) for at, source in enumerate((k, v, q, og))]
    for move in moves:
        move.start()
    rows = id_rows_of(ids)
    rows.append(jnp.zeros((16 - len(rows), 128), F32))
    rows = jnp.concatenate(rows, axis=0).astype(BF16)
    for d in range(G):
        outs[d][3 * BL : 3 * BL + 16] = rows
    for at, move in enumerate(moves[:3]):
        move.wait()
        for d in range(G):
            cols = pl.ds(pl.multiple_of((g ^ d) * HD, HD), HD)
            outs[d][at * BL : (at + 1) * BL] = held[at, :, cols]
    moves[3].wait()
    route_grads(sizes, held[3], gates, ids, sent)


def upper_body(sizes, og, *refs):
    G, R, BL = sizes
    outs, sems = refs[:G], refs[G]
    g = lax.axis_index("seq") // R
    moves = []
    for d in range(G):
        cols = pl.ds(pl.multiple_of((g ^ d) * HD, HD), HD)
        moves.append(pltpu.make_async_copy(og.at[:, cols], outs[d], sems.at[d]))
    for move in moves:
        move.start()
    for move in moves:
        move.wait()


def route_grads(sizes, block, gates, ids, outs):
    G, R, BL, cap, stride = sizes
    n = G * R
    slots = relative_slots(id_rows_of(ids), lax.axis_index("seq"), n, cap, stride)
    routing = lax.broadcasted_iota(jnp.int32, (n * stride, 2 * BL), 0) == slots
    diagonal = lax.broadcasted_iota(jnp.int32, (BL, BL), 0) == lax.broadcasted_iota(jnp.int32, (BL, BL), 1)
    block = block.astype(F32)
    scaled = []
    for j in range(2):
        gate = jnp.sum(jnp.where(diagonal, gates[j : j + 1], 0.0), axis=1, keepdims=True)
        scaled.append((gate * block).astype(BF16))
    routed = plain(routing.astype(F32).astype(BF16), jnp.concatenate(scaled, axis=0)).astype(BF16)
    for dg in range(G):
        for dr in range(R):
            d = dg * R + dr
            outs[dr][dg * stride : (dg + 1) * stride] = routed[d * stride : (d + 1) * stride]


def routing_body(sizes, *refs):
    G, R, BL, cap, stride = sizes
    n = G * R
    s = lax.axis_index("seq")
    own, out = refs[:G], refs[G]
    for d in range(G):
        rows = own[d][...].astype(F32)
        slots = relative_slots([rows[k : k + 1] for k in range(2 * BL // 128)], s, n, cap, stride)
        slot_rows = lax.broadcasted_iota(jnp.int32, (n * stride, BL), 0)
        chosen = (slot_rows == slots[:, :BL]) | (slot_rows == slots[:, BL:])
        out[pl.ds((s // R) ^ d, 1)] = chosen.astype(F32).astype(BF16)[None]


def pair_groups(G):
    return [members for members in ([0], list(range(1, G))) if members and members[-1] < G]


def forward_body(sizes, slopes, *refs):
    G, R, BL, cap, stride = sizes
    n = G * R
    total = n * BL
    s = lax.axis_index("seq")
    g, r = s // R, s % R
    own, refs = refs[:G], refs[G:]
    groups = pair_groups(G)
    others, refs = refs[: len(groups) * (R - 1)], refs[len(groups) * (R - 1) :]
    far, refs = refs[: G + 4], refs[G + 4 :]
    attn_out, refs = refs[0], refs[1:]
    near, sems = refs[: G + 4], refs[G + 4]
    probs = near[:G]
    attn, keys, values, queries = near[G:]

    def kept(at):
        return pltpu.make_async_copy(near[at], far[at], sems.at[at])

    for d in range(G):
        i = g ^ d
        queries[pl.ds(pl.multiple_of(i * BL, BL), BL)] = own[d][2 * BL : 3 * BL]
        for dr in range(R):
            piece, at = own[d], 0
            if dr:
                group = next(k for k, members in enumerate(groups) if d in members)
                piece = others[(dr - 1) * len(groups) + group]
                at = groups[group].index(d) * 2 * BL
            rows = pl.ds(pl.multiple_of((i * R + (r ^ dr)) * BL, BL), BL)
            keys[rows] = piece[at : at + BL]
            values[rows] = piece[at + BL : at + 2 * BL]
    for at in range(G + 1, G + 4):
        kept(at).start()
    slope = slopes[g]
    span = R * BL
    for i in range(G):
        N = (i + 1) * span
        scores = rows_by_rows(queries[i * BL : (i + 1) * BL], keys[0:N])
        col = lax.broadcasted_iota(jnp.int32, (1, N), 1)
        bias = (col - N).astype(F32) * (slope * LOG2E)
        scores = scores * (HD**-0.5 * LOG2E) + bias
        if total > WCH * BL:
            distance = (
                lax.broadcasted_iota(jnp.int32, (BL, N), 0) + (i * R + r) * BL - lax.broadcasted_iota(jnp.int32, (BL, N), 1)
            )
            scores = jnp.where((distance >= 0) & (distance < WCH * BL), scores, -jnp.inf)
        else:
            ahead = lax.broadcasted_iota(jnp.int32, (BL, span), 1) - lax.broadcasted_iota(jnp.int32, (BL, span), 0)
            last = jnp.where(ahead <= r * BL, scores[:, N - span :], -jnp.inf)
            scores = last if i == 0 else jnp.concatenate([scores[:, : N - span], last], axis=1)
        top = jnp.max(scores, axis=1, keepdims=True)
        grown = jnp.exp2(scores - top)
        norm = jnp.sum(grown, axis=1, keepdims=True)
        weights = (grown * (1.0 / norm)).astype(BF16)
        probs[i][...] = weights
        kept(i).start()
        out = plain(weights, values[0:N]).astype(BF16)
        attn[i * BL : (i + 1) * BL] = out
        attn_out[i * BL : (i + 1) * BL] = out
    kept(G).start()
    for at in range(G + 4):
        kept(at).wait()


def dispatch_body(sizes, attn, routing, *sent):
    G, R, BL, cap, stride = sizes
    for i in range(G):
        routed = plain(routing[i], attn[i * BL : (i + 1) * BL]).astype(BF16)
        for dg in range(G):
            for dr in range(R):
                d = dg * R + dr
                at = (dr * G + i) * stride
                sent[dg][at : at + stride] = routed[d * stride : (d + 1) * stride]


def spread(sizes, total, outs):
    G, R, BL = sizes[:3]
    s = lax.axis_index("seq")
    g, r = s // R, s % R
    for d in range(G):
        for dr in range(R):
            rows = pl.ds(pl.multiple_of(((g ^ d) * R + (r ^ dr)) * BL, BL), BL)
            outs[dr][d * BL : (d + 1) * BL] = total[rows].astype(BF16)


def backward_body(sizes, *refs):
    G, R, BL, cap, stride = sizes
    n = G * R
    g = lax.axis_index("seq") // R
    back, refs = refs[:n], refs[n:]
    upper, refs = refs[:G], refs[G:]
    probs, refs = refs[:G], refs[G:]
    routing, attn, keys, values, queries, refs = *refs[:5], refs[5:]
    query_out, refs = refs[:G], refs[G:]
    value_out, key_out, refs = refs[:R], refs[R : 2 * R], refs[2 * R :]
    upper_rows, query_rows, value_sum, key_sum = refs
    scale = HD**-0.5
    for d in range(G):
        upper_rows[pl.ds(pl.multiple_of((g ^ d) * BL, BL), BL)] = upper[d][...]
    for i in reversed(range(G)):
        N = (i + 1) * R * BL
        mine = slice(i * BL, (i + 1) * BL)
        rows = jnp.concatenate([back[d][i * stride : (i + 1) * stride] for d in range(n)], axis=0)
        picked = cols_by_cols(routing[i], rows)
        grad = (upper_rows[mine].astype(F32) + picked).astype(BF16)
        weights = probs[i][...]
        value_part = cols_by_cols(weights, grad)
        delta = jnp.sum(grad.astype(F32) * attn[mine].astype(F32), axis=1, keepdims=True)
        dprob = rows_by_rows(grad, values[0:N])
        dscore = (weights.astype(F32) * (dprob - delta)).astype(BF16)
        query_rows[mine] = (plain(dscore, keys[0:N]) * scale).astype(BF16)
        key_part = cols_by_cols(dscore, queries[mine]) * scale
        if i == G - 1:
            value_sum[...] = value_part
            key_sum[...] = key_part
        else:
            value_sum[0:N] += value_part
            key_sum[0:N] += key_part
    for d in range(G):
        query_out[d][...] = query_rows[pl.ds(pl.multiple_of((g ^ d) * BL, BL), BL)]
    spread(sizes, value_sum, value_out)
    spread(sizes, key_sum, key_out)


def unpack_body(sizes, *refs):
    G, R, BL = sizes
    g = lax.axis_index("seq") // R
    pieces, outs = refs[: 3 * G], refs[3 * G :]
    for at in range(3):
        for d in range(G):
            cols = pl.ds(pl.multiple_of((g ^ d) * HD, HD), HD)
            outs[at][:, cols] = pieces[at * G + d][...]


def turn_tokens_body(sizes, *refs):
    G, R, count = sizes
    g = lax.axis_index("seq") // R
    for dg in range(G):
        cols = pl.ds(pl.multiple_of((g ^ dg) * HD, HD), HD)
        for dr in range(R):
            refs[G + dr][:, cols] = refs[dg][dr * count : (dr + 1) * count]


def column_body(sizes, *refs):
    G, R, stride = sizes
    for dg in range(G):
        for dr in range(R):
            refs[R + dg][dr * stride : (dr + 1) * stride] = refs[dr][dg * stride : (dg + 1) * stride]


def turn_grads_body(sizes, *refs):
    G, R, stride = sizes
    g = lax.axis_index("seq") // R
    for dg in range(G):
        for dr in range(R):
            at = pl.ds(pl.multiple_of((dr * G + (g ^ dg)) * stride, 16), stride)
            refs[-1][at] = refs[dg][dr * stride : (dr + 1) * stride]


def turn_back_body(sizes, start, arrived, *refs):
    G, R, count = sizes
    g = lax.axis_index("seq") // R
    each = arrived.shape[0] // count
    near, outs = refs[: len(refs) - G * each], refs[len(refs) - G * each :]
    for dg in range(G):
        cols = pl.ds(pl.multiple_of((g ^ dg) * HD, HD), HD)
        for at in range(each):
            total = arrived[at * count : (at + 1) * count, cols].astype(F32)
            for piece in near:
                total = total + piece[start + at * count : start + (at + 1) * count, cols].astype(F32)
            outs[dg * each + at][...] = total.astype(BF16)


def keep_moves(parts, first, shards, full, sems):
    place = lax.axis_index("exp")
    rows, width = shards[0].shape
    moves = []
    for at, shard in enumerate(shards):
        k, h = first + at // parts, at % parts
        cols = pl.ds(pl.multiple_of((place ^ k) * width, 128), width)
        moves.append(pltpu.make_async_copy(shard, full.at[pl.ds(h * rows, rows), cols], sems.at[at]))
    return moves


def through_body(parts, weight, *refs):
    shards, out, full, held, sems, own_sems = refs[:-5], *refs[-5:]
    place = lax.axis_index("exp")
    rows, width = shards[0].shape
    steps = sems.shape[0]
    kept = keep_moves(parts, 0, shards, full, own_sems)
    tall = weight.shape[0] // steps

    def fetch(c):
        mine = pl.ds(c * tall, tall)
        return pltpu.make_async_copy(weight.at[mine], held.at[mine], sems.at[c])

    for c in range(min(2, steps)):
        fetch(c).start()
    for move in kept:
        move.start()
    for c in range(steps):
        fetch(c).wait()
        if c + 2 < steps:
            fetch(c + 2).start()
        for h in range(parts):
            total = None
            for k in range(len(shards) // parts):
                cols = pl.ds(pl.multiple_of((place ^ k) * width, 128), width)
                part = rows_by_rows(shards[k * parts + h][...], held[c * tall : (c + 1) * tall, cols])
                total = part if total is None else total + part
            out[h * rows : (h + 1) * rows, c * tall : (c + 1) * tall] = total
    for move in kept:
        move.wait()


def pre_body(parts, weight, *refs):
    held, sems, own_sems = refs[-3:]
    count = (len(refs) - 7) // (parts + 1)
    shards, refs = refs[: count * parts], refs[count * parts : -3]
    through, full, hidden, hidden_grad, back = *refs[:4], refs[4:]
    place = lax.axis_index("exp")
    rows, width = shards[0].shape
    steps = sems.shape[0]
    wide = weight.shape[1] // steps
    kept = keep_moves(parts, 0, shards, full, own_sems)

    def fetch(c, k):
        at = pl.ds(pl.multiple_of((place ^ k) * width, 128), width)
        return pltpu.make_async_copy(weight.at[at, pl.ds(c * wide, wide)], held.at[c, at], sems.at[c, k])

    for c in range(min(2, steps)):
        for k in range(count):
            fetch(c, k).start()
    for c in range(steps):
        cols = slice(c * wide, (c + 1) * wide)
        if c + 2 < steps:
            for k in range(count):
                fetch(c + 2, k).start()
        for h in range(parts):
            mine = slice(h * rows, (h + 1) * rows)
            total = None
            for k in range(len(shards) // parts):
                at = pl.ds(pl.multiple_of((place ^ k) * width, 128), width)
                if h == 0:
                    fetch(c, k).wait()
                part = plain(shards[k * parts + h][...], held[c, at, :])
                total = part if total is None else total + part
            logistic = 1.0 / (1.0 + jnp.exp(-total))
            hidden[mine, cols] = (total * logistic).astype(BF16)
            grad = through[mine, cols] * logistic * (1.0 + total * (1.0 - logistic))
            hidden_grad[mine, cols] = grad.astype(BF16)
        if c == 0:
            for move in kept:
                move.start()
    for k, out in enumerate(back):
        at = pl.ds(pl.multiple_of((place ^ k) * width, 128), width)
        total = None
        for c in range(steps):
            part = rows_by_rows(hidden_grad[:, c * wide : (c + 1) * wide], held[c, at, :])
            total = part if total is None else total + part
        out[...] = total.astype(out.dtype)
    for move in kept:
        move.wait()


def far_body(kept, moved, *outs):
    rows = outs[0].shape[0]
    for h, out in enumerate(outs):
        mine = slice(h * rows, (h + 1) * rows)
        out[...] = (kept[mine] + moved[mine].astype(F32)).astype(BF16)


def weight_grad_body(place, left, right, out, mark):
    mark[...] = jnp.zeros_like(mark)
    out[...] = cols_by_cols(left[...], right[...]).astype(BF16)


def gather_exp(block, size):
    distance = size // 2
    by_place = {0: block}
    while distance:
        for place in list(by_place):
            by_place[place ^ distance] = swap(by_place[place], "exp", distance)
        distance //= 2
    return [by_place[k] for k in range(size)]


def per_device(
    queries,
    key_rows,
    value_rows,
    out_grad,
    expert_ids,
    gate_values,
    alibi_slope,
    expert_in,
    expert_out,
):
    BL, features = queries.shape
    G = features // HD
    n = lax.axis_size("seq")
    E = lax.axis_size("exp")
    R = n // G
    cap = 5 * BL // (2 * n)
    stride = -(-cap // 16) * 16
    rows = n * stride
    FFL = expert_in.shape[2]
    L = n * BL
    parts = 2
    each = R // parts
    tall = rows // parts
    half = E // 2
    sizes = (G, R, BL, cap, stride)
    limit = attention_limit(BL, L)
    weight_in = expert_in[0]
    weight_out = expert_out[0]

    ids, gates = expert_ids.T, gate_values.T
    arrays_of = lambda arrays: [
        arrays[h * each] if each == 1 else jnp.concatenate(arrays[h * each : (h + 1) * each], axis=0) for h in range(parts)
    ]

    made = local_call(
        functools.partial(pack_body, sizes),
        [((3 * BL + 16, HD), BF16)] * G + [((G * stride, features), BF16)] * R + [((1,), jnp.int32, pltpu.SMEM)],
        [ids, gates],
        far=[queries, key_rows, value_rows, out_grad],
        scratch=[pltpu.VMEM((4, BL, features), BF16), pltpu.SemaphoreType.DMA((4,))],
        limit=57 * MIB,
        nbytes=6 * BL * features * 2,
    )
    place = made[G + R]
    grad_sent = [swap(made[G + dr], "seq", dr) for dr in range(R)]
    own = [swap(made[d], "seq", d * R) for d in range(G)]
    pairs = [
        own[members[0]][: 2 * BL] if len(members) == 1 else jnp.concatenate([own[d][: 2 * BL] for d in members], axis=0)
        for members in pair_groups(G)
    ]
    others = [swap(piece, "seq", dr) for dr in range(1, R) for piece in pairs]
    block = ((16, HD), (3 * BL // 16, 0))
    routing = local_call(
        functools.partial(routing_body, sizes),
        [((G, rows, BL), BF16)],
        [(own[d], *block) for d in range(G)],
        flops=2 * G * 8 * 4 * BL * BL,
        nbytes=rows * BL * G * 2,
    )[0]

    grad_pieces = local_call(
        functools.partial(column_body, (G, R, stride)),
        [((R * stride, features), BF16)] * G,
        grad_sent,
        after=own[1:],
        nbytes=rows * features * 4,
    )
    kept = [((BL, (i + 1) * R * BL), BF16, pltpu.HBM) for i in range(G)]
    kept += [(shape, BF16, pltpu.HBM) for shape in ((G * BL, HD), (L, HD), (L, HD), (G * BL, HD))]
    shapes = kept + [((G * BL, HD), BF16)]
    made = local_call(
        functools.partial(forward_body, sizes),
        shapes,
        own + others,
        scalars=[alibi_slope],
        scratch=[pltpu.VMEM(x[0], x[1]) for x in kept] + [pltpu.SemaphoreType.DMA((G + 4,))],
        flops=0,
        nbytes=0,
        limit=limit,
    )
    probs = list(made[:G])
    attn, keys, values, query_rows = made[G : G + 4]
    token_sent = local_call(
        functools.partial(dispatch_body, sizes),
        [((R * G * stride, HD), BF16)] * G,
        [made[G + 4], routing],
        flops=2 * rows * BL * HD * G,
        nbytes=2 * MIB,
    )
    grads = local_call(
        functools.partial(turn_grads_body, (G, R, stride)),
        [((rows, features), BF16)],
        [swap(grad_pieces[dg], "seq", dg * R) for dg in range(G)],
        after=token_sent[:1],
        nbytes=rows * features * 4,
    )[0]
    grads_far = swap(grads, "exp", half)
    token_pieces = [swap(token_sent[dg], "seq", dg * R) for dg in range(G)]
    grad_shards = gather_exp(grads, half) + gather_exp(hold([grads_far], token_pieces[1:] or token_pieces)[0], half)
    width = min(256, FFL)
    steps = FFL // width
    whole = lambda array: (array, array.shape, lambda j, p: (0, 0))
    column_of = lambda array: (array, (array.shape[0], width), lambda j, p: (0, j))
    work = 2 * rows * FFL * features
    through, full_grads = local_call(
        functools.partial(through_body, 1),
        [((rows, FFL), F32), ((rows, E * features), BF16, pltpu.HBM)],
        grad_shards,
        far=[weight_out],
        scratch=[
            pltpu.VMEM((FFL, E * features), BF16),
            pltpu.SemaphoreType.DMA((steps,)),
            pltpu.SemaphoreType.DMA((E,)),
        ],
        flops=work * E,
        nbytes=10 * MIB,
    )

    tokens = local_call(
        functools.partial(turn_tokens_body, (G, R, G * stride)),
        [((G * stride, features), BF16)] * R,
        token_pieces,
        after=[grads_far],
        nbytes=rows * features * 4,
    )
    token_parts = arrays_of([swap(tokens[dr], "seq", dr) for dr in range(R)])
    token_parts[1:] = hold(token_parts[1:], [through])
    upper = local_call(
        functools.partial(upper_body, (G, R, BL)),
        [((BL, HD), BF16)] * G,
        [],
        after=token_parts[1:],
        far=[out_grad],
        scratch=[pltpu.SemaphoreType.DMA((G,))],
        nbytes=2 * BL * features * 2,
    )
    upper = [swap(upper[d], "seq", d * R) for d in range(G)]
    far_parts = [swap(part, "exp", half) for part in token_parts]
    if G > 1:
        far_parts[1:] = hold(far_parts[1:], upper[1:])
    near_shards = [gather_exp(part, half) for part in token_parts]
    near_shards = [near_shards[h][k] for k in range(half) for h in range(parts)]
    far_shards = [gather_exp(part, half) for part in far_parts]
    far_shards = [far_shards[h][k] for k in range(half) for h in range(parts)]
    full_tokens, hidden, hidden_grad, *back = local_call(
        functools.partial(pre_body, parts),
        [((rows, E * features), BF16, pltpu.HBM)]
        + [((rows, FFL), BF16)] * 2
        + [((rows, features), BF16 if k % 2 else F32) for k in range(E)],
        near_shards + far_shards + [through],
        far=[weight_in],
        scratch=[
            pltpu.VMEM((steps, E * features, width), BF16),
            pltpu.SemaphoreType.DMA((steps, E)),
            pltpu.SemaphoreType.DMA((E * parts,)),
        ],
        flops=2 * work * E,
        nbytes=8 * MIB,
        limit=20 * MIB,
    )

    moved = [swap(back[k], "exp", 1) for k in range(1, E, 2)]
    kept = back[::2]
    pairs = half // 2
    far = [
        local_call(far_body, [((tall, features), BF16)] * parts, [kept[k], moved[k]], nbytes=rows * features * 8)
        for k in range(pairs, 2 * pairs)
    ]
    arrived = [[swap(piece[h], "exp", half) for h in range(parts)] for piece in far]
    near = [[kept[k], moved[k]] for k in range(pairs)]
    distance = half // 2
    while len(near) > 1:
        count = len(near) // 2
        total = [sum(x.astype(F32) for x in near[k]) + jnp.concatenate(arrived[k], axis=0) for k in range(2 * count)]
        sent = [total[count + k].astype(BF16) for k in range(count)]
        arrived = [[swap(x[h * tall : (h + 1) * tall], "exp", distance) for h in range(parts)] for x in sent]
        near = [[x] for x in total[:count]]
        distance //= 2

    mark_out = ((8, 128), F32, (8, 128), lambda j, p: (0, 0))
    out_weight_grad, out_mark = grid_call(
        weight_grad_body,
        steps,
        place,
        [column_of(hidden), whole(full_grads)],
        [((FFL, features * E), BF16, (width, features * E), lambda j, p: (j, 0)), mark_out],
        flops=work * E,
        nbytes=10 * MIB,
    )
    returned = [None] * n
    ready = [out_mark]
    for h in range(parts):
        pieces = local_call(
            functools.partial(turn_back_body, (G, R, G * stride), h * tall),
            [((G * stride, HD), BF16)] * (G * each),
            [arrived[0][h]] + near[0],
            after=ready,
            nbytes=tall * features * 8,
        )
        for dg in range(G):
            for at in range(each):
                d = dg * R + h * each + at
                returned[d] = swap(pieces[dg * each + at], "seq", d)
        ready = returned[R : R + 1]
    in_weight_grad, in_mark = grid_call(
        weight_grad_body,
        E,
        place,
        [(full_tokens, (rows, features), lambda j, p: (0, j)), whole(hidden_grad)],
        [((features * E, FFL), BF16, (features, FFL), lambda j, p: (j, 0)), mark_out],
        flops=work * E,
        nbytes=10 * MIB,
    )

    made = local_call(
        functools.partial(backward_body, sizes),
        [((BL, HD), BF16)] * G + [((G * BL, HD), BF16)] * (2 * R),
        returned + upper + probs + [routing, attn, keys, values, query_rows],
        after=[in_mark],
        scratch=[
            pltpu.VMEM((G * BL, HD), BF16),
            pltpu.VMEM((G * BL, HD), BF16),
            pltpu.VMEM((L, HD), F32),
            pltpu.VMEM((L, HD), F32),
        ],
        flops=8 * G * BL * L * HD,
        nbytes=10 * MIB,
        limit=limit,
    )
    query_pieces, value_parts, key_parts = made[:G], made[G : G + R], made[G + R :]

    def home(pair_parts):
        moved = [swap(pair_parts[dr], "seq", dr) for dr in range(1, R)]
        pieces = []
        for d in range(G):
            mine = slice(d * BL, (d + 1) * BL)
            total = pair_parts[0][mine].astype(F32)
            for piece in moved:
                total = total + piece[mine].astype(F32)
            pieces.append(swap(total.astype(BF16), "seq", d * R))
        return pieces

    value_home = home(value_parts)
    query_home = [swap(query_pieces[d], "seq", d * R) for d in range(G)]
    key_home = home(key_parts)
    query_grad, key_grad, value_grad = local_call(
        functools.partial(unpack_body, (G, R, BL)),
        [((BL, features), BF16)] * 3,
        query_home + key_home + value_home,
        nbytes=6 * BL * features * 2,
    )
    return query_grad, key_grad, value_grad, in_weight_grad[None], out_weight_grad[None]


def solution(mesh):
    return jax.shard_map(
        per_device,
        mesh=mesh,
        in_specs=(
            P("seq", "exp"),
            P("seq", "exp"),
            P("seq", "exp"),
            P("seq", "exp"),
            P("seq", None),
            P("seq", None),
            P("exp"),
            P("seq", None, "exp"),
            P("seq", "exp", None),
        ),
        out_specs=(
            P("seq", "exp"),
            P("seq", "exp"),
            P("seq", "exp"),
            P("seq", None, "exp"),
            P("seq", "exp", None),
        ),
        check_vma=False,
    )
```
